512 devices in a mesh: batch: 4 (over y_hi), ctx: 128 (over x, z, y_lo, core).
Axes of the slice: x: 4, y: 8 (y_hi: 4, y_lo: 2; y = y_hi * 2 + y_lo), z: 8, core: 2. Of those that a mesh axis runs over, the one named last changes fastest.
Arguments:
- queries: bfloat16 [4, 32768, 1024], P('batch', 'ctx'), may hold values from -6 to 6
- keys: bfloat16 [4, 32768, 1024], P('batch', 'ctx'), may hold values from -6 to 6
- values: bfloat16 [4, 32768, 1024], P('batch', 'ctx'), may hold values from -6 to 6
- gates: bfloat16 [4, 32768, 1024], P('batch', 'ctx'), may hold values from -6 to 6
- cotangent: bfloat16 [4, 32768, 1024], P('batch', 'ctx'), may hold values from -6 to 6
- rel_bias: float32 [8, 32], replicated, may hold values from -2 to 2
- lengths: int32 [4, 16], P('batch'), may hold values from 1 to 8192, 32768 in all within a row
- send_counts: int32 [4, 128, 128], P('batch'), may hold values from 0 to 3, as said below
- block_pattern: int32 [4, 256, 2], P('batch', 'ctx'), may hold values from 0 to 1, as said below
Outputs:
- query_grad: bfloat16 [4, 32768, 1024], P('batch', 'ctx')
- key_grad: bfloat16 [4, 32768, 1024], P('batch', 'ctx')
- value_grad: bfloat16 [4, 32768, 1024], P('batch', 'ctx')
- gate_grad: bfloat16 [4, 32768, 1024], P('batch', 'ctx')
- bias_grad: float32 [8, 32], replicated
The draws below stay inside these ranges and needn't reach their ends.
Inputs may be any that keep to these rules, and one draw needn't show every extreme that they name: Every loader's row of send_counts[g] and every owner's column sums to 256; every loader hands exactly 3 rows to some owner and every owner receives exactly 3 rows from some loader. `block_pattern`: entry j of a query block's row says whether it attends the block j blocks back; entry 0 is always 1. The 16 lengths of a group sum to 32768; the longest is exactly 8192.
All inputs are finite; a program needn't handle non-finite values.
Results may differ from the reference program's by a relative error of at most 0.0058.
Values may be sent and summed in bfloat16 or wider, within the bound.
A program may use at most 64 MiB of HBM per device.

```python
import math
import jax
import jax.numpy as jnp
import numpy as np
from jax import lax

D = 1024
HEADS = 8
BLOCK = 128
WIN_BLK = 2
BUCKETS = 32
HIST = 16
BLK_DEV = 2
EVENTS_DEV = 256
N_BLK = 256
EVENTS = 32768
GROUPS = 4
N_CTX = 128


def draw_send_counts(key, part):
    key = jax.random.fold_in(key, 11)
    half = EVENTS_DEV // (2 * N_CTX)
    base = 2 * half

    def one_group(sub):
        first, second, third = jax.random.split(sub, 3)
        signs = jax.random.randint(first, (N_CTX // 2,), -1, 2)
        signs = signs.at[0].set(1)
        offsets_table = jnp.stack([signs, -signs], axis=1).reshape(-1)
        owner_perm = jax.random.permutation(second, N_CTX)
        loader_perm = jax.random.permutation(third, N_CTX)
        offsets = (owner_perm[None, :] - loader_perm[:, None]) % N_CTX
        return base + half * offsets_table[offsets]
    return jax.vmap(one_group)(jax.random.split(key, GROUPS)).astype(jnp.int32)


def draw_block_pattern(key, part):
    key = jax.random.fold_in(key, 23)
    first, second = jax.random.split(key)
    level = jax.random.randint(first, (GROUPS, N_CTX, 1, 1), 1, 9)
    coins = jax.random.randint(second, (GROUPS, N_CTX, BLK_DEV, WIN_BLK), 0, 8)
    flags = (coins < level).astype(jnp.int32)
    flags = flags.at[..., 0].set(1)
    return flags.reshape(GROUPS, N_CTX * BLK_DEV, WIN_BLK)


def levels(stream_key, extent, shards, smallest, high):
    gain = 1.0
    for position, parts in shards:
        steps = jax.random.uniform(jax.random.fold_in(jax.random.fold_in(stream_key, 6), position), (parts,), jnp.float32, smallest / len(shards), high / len(shards))
        gain = gain * jnp.repeat(jnp.exp(steps), extent[position] // parts).reshape((-1,) + (1,) * (len(extent) - 1 - position))
    return gain


def split_up(amount, total, reach, skew):
    weights = [(1 << 20) // math.isqrt(standing ** skew) + 1 for standing in range(2, amount + 1)]
    spare, counts = total - reach - (amount - 1), [1] * (amount - 1)
    while spare > 0:
        movable = [i for i in range(amount - 1) if counts[i] < reach]
        pool, budget = sum([weights[i] for i in movable]), spare
        for i in movable:
            more = min(reach - counts[i], max(1, budget * weights[i] // pool), spare)
            counts[i] = counts[i] + more
            spare = spare - more
    return np.array([reach] + counts)


def ragged_sizes(stream_key, amount, total, most, slope):
    if amount == 2:
        one = jax.random.randint(stream_key, (), max(1, total - most), min(most, total - 1) + 1)
        return jnp.stack([one, total - one])
    sizes = jnp.asarray(split_up(amount, total, most, slope), jnp.int32)
    couples = (amount - 1) // 2
    giver, sink = sizes[1:1 + 2 * couples:2], sizes[2:2 + 2 * couples:2]
    room = jnp.minimum(giver - 1, most - sink)
    passed = jax.random.randint(jax.random.fold_in(stream_key, 1), (couples,), 0, 1 << 20) % (room + 1)
    sizes = sizes.at[1:1 + 2 * couples:2].set(giver - passed).at[2:2 + 2 * couples:2].set(sink + passed)
    return sizes[jax.random.permutation(jax.random.fold_in(stream_key, 2), amount)]


def noise(stream_key, shape, spread, most, shards=(), held_as=jnp.bfloat16):
    values = spread * jax.random.normal(stream_key, shape, jnp.float32)
    if shards:
        values = values * levels(stream_key, shape, shards, -0.22, 0.18)
    return jnp.clip(values, -most, most).astype(held_as)


def setup_inputs(seed: int = 0) -> dict:
    arg_keys = jax.random.split(jax.random.key(seed), 10)
    queries = noise(arg_keys[0], (GROUPS, EVENTS, D), 1.0, 6.0, ((0, 4), (1, 128)))
    keys = noise(arg_keys[1], (GROUPS, EVENTS, D), 1.0, 6.0, ((0, 4), (1, 128)))
    values = noise(arg_keys[2], (GROUPS, EVENTS, D), 1.0, 6.0, ((0, 4), (1, 128)))
    gates = noise(arg_keys[3], (GROUPS, EVENTS, D), 1.0, 6.0, ((0, 4), (1, 128)))
    cotangent = noise(arg_keys[4], (GROUPS, EVENTS, D), 1.0, 6.0, ((0, 4), (1, 128)))
    rel_bias = jnp.clip(jax.random.uniform(arg_keys[5], (HEADS, BUCKETS), jnp.float32, -2.0, 2.0), -2.0, 2.0)
    lengths = jax.vmap(lambda own: ragged_sizes(own, HIST, EVENTS, EVENTS // 4, 2))(jax.random.split(arg_keys[6], GROUPS)).reshape((GROUPS, HIST)).astype(jnp.int32)
    send_counts = draw_send_counts(jax.random.fold_in(arg_keys[9], 71), 0)
    block_pattern = draw_block_pattern(jax.random.fold_in(arg_keys[9], 71), 0)
    return {"queries": queries, "keys": keys, "values": values, "gates": gates, "cotangent": cotangent, "rel_bias": rel_bias, "lengths": lengths, "send_counts": send_counts, "block_pattern": block_pattern}


EPS = 1e-05
HIGH = lax.Precision.HIGHEST

def segment_of(places, ends):
    return lax.optimization_barrier(jnp.sum((places[..., None] >= ends).astype(jnp.int32), axis=-1))

def window_mask(starts, flags, ends, key_limit, block, window):
    offsets = jnp.arange(block, dtype=jnp.int32)
    place_q = starts[:, None] + offsets[None, :]
    moves = (jnp.arange(window, dtype=jnp.int32) - (window - 1)) * block
    place_k = starts[:, None, None] + moves[None, :, None] + offsets[None, None, :]
    hist_q = segment_of(place_q, ends)
    hist_k = segment_of(place_k, ends)
    live = (place_k[:, None] <= place_q[:, :, None, None]) & (place_k[:, None] >= 0)
    live = live & (place_k[:, None] < key_limit) & (hist_k[:, None] == hist_q[:, :, None, None])
    return live.astype(jnp.float32) * flags[:, ::-1][:, None, :, None]

def bias_table(rel_bias, block, window):
    buckets = rel_bias.shape[1]
    span = window * block
    grid = (block, window, block)
    row_i = lax.broadcasted_iota(jnp.int32, grid, 0)
    slot_w = lax.broadcasted_iota(jnp.int32, grid, 1)
    col_c = lax.broadcasted_iota(jnp.int32, grid, 2)
    distance = jnp.clip(row_i + (window - 1 - slot_w) * block - col_c, 0, span - 1)
    bucket = (distance * buckets // span).reshape(-1)
    onehot = (jnp.arange(buckets, dtype=jnp.int32)[:, None] == bucket[None, :]).astype(jnp.float32)
    full = jnp.einsum('hk,kp->hp', rel_bias, onehot, precision=HIGH)
    return (full.reshape(rel_bias.shape[0], block, window, block), onehot)

def windows(ext_rows, count, block, window):
    pieces = ext_rows.reshape(-1, block, ext_rows.shape[-1])
    return jnp.stack([pieces[w:w + count] for w in range(window)], axis=1)

def fold_window(terms):
    count, window, block, width = terms.shape
    total = jnp.zeros((count + window - 1, block, width), jnp.float32)
    for w in range(window):
        total = total + jnp.pad(terms[:, w], ((w, window - 1 - w), (0, 0), (0, 0)))
    return total.reshape(-1, width)

def attend_forward(query_blocks, key_win, value_win, mask, bias_full):
    heads = bias_full.shape[0]
    count, block, width = query_blocks.shape
    window = key_win.shape[1]
    size = width // heads
    mask_scaled = mask * (1.0 / (window * block))
    query_heads = query_blocks.reshape(count, block, heads, size).astype(jnp.float32)
    key_heads = key_win.reshape(count, window, block, heads, size).astype(jnp.float32)
    value_heads = value_win.reshape(count, window, block, heads, size).astype(jnp.float32)
    scores = jnp.einsum('nrhd,nwchd->nhrwc', query_heads, key_heads) * size ** (-0.5) + bias_full[None]
    weights = (jax.nn.silu(scores) * mask_scaled[:, None]).astype(jnp.bfloat16)
    output = jnp.einsum('nhrwc,nwchd->nrhd', weights.astype(jnp.float32), value_heads)
    return (scores, weights, output.reshape(count * block, width))

def attend_backward(query_blocks, key_win, value_win, mask, scores, weights, grad_blocks, heads):
    count, block, width = query_blocks.shape
    window = key_win.shape[1]
    size = width // heads
    mask_scaled = mask * (1.0 / (window * block))
    query_heads = query_blocks.reshape(count, block, heads, size).astype(jnp.float32)
    key_heads = key_win.reshape(count, window, block, heads, size).astype(jnp.float32)
    value_heads = value_win.reshape(count, window, block, heads, size).astype(jnp.float32)
    grad_heads = grad_blocks.reshape(count, block, heads, size).astype(jnp.float32)
    grad_weights = jnp.einsum('nrhd,nwchd->nhrwc', grad_heads, value_heads)
    gate_sig = jax.nn.sigmoid(scores)
    grad_scores = grad_weights * (gate_sig * (1.0 + scores * (1.0 - gate_sig))) * mask_scaled[:, None]
    grad_low = grad_scores.astype(jnp.bfloat16).astype(jnp.float32)
    scale = size ** (-0.5)
    query_grad = jnp.einsum('nhrwc,nwchd->nrhd', grad_low, key_heads) * scale
    key_grad = jnp.einsum('nhrwc,nrhd->nwchd', grad_low, query_heads) * scale
    value_grad = jnp.einsum('nhrwc,nrhd->nwchd', weights.astype(jnp.float32), grad_heads)
    return (grad_scores, query_grad.reshape(count * block, width), key_grad.reshape(count, window, block, width), value_grad.reshape(count, window, block, width))

def norm_parts(output):
    center = output - lax.optimization_barrier(jnp.mean(output, axis=-1, keepdims=True))
    inverse = lax.rsqrt(lax.optimization_barrier(jnp.mean(center * center, axis=-1, keepdims=True)) + EPS)
    return (center * inverse, inverse)

def norm_back(grad_normed, normed, inverse):
    return (grad_normed - lax.optimization_barrier(jnp.mean(grad_normed, axis=-1, keepdims=True)) - normed * lax.optimization_barrier(jnp.mean(grad_normed * normed, axis=-1, keepdims=True))) * inverse

def owner_sources(table):
    row_start = jnp.cumsum(table, axis=1) - table
    col_incl = jnp.cumsum(table, axis=0)
    col_excl = col_incl - table
    places = jnp.arange(EVENTS_DEV, dtype=jnp.int32)
    loader = lax.optimization_barrier(jnp.sum((col_incl[:, :, None] <= places[None, None, :]).astype(jnp.int32), axis=0))
    loader_t = loader.T
    excl_at = jnp.take_along_axis(col_excl, loader_t, axis=0)
    start_at = jnp.take_along_axis(row_start, loader_t, axis=0)
    source = loader_t * EVENTS_DEV + start_at + places[:, None] - excl_at
    return source.T.reshape(-1).astype(jnp.int32)

def group_pass(arrays, bias_full, onehot):
    queries, keys, values, gates, cotangent, lengths, table, pattern = arrays
    sources = owner_sources(table)
    query_own = queries[sources]
    key_own = keys[sources]
    value_own = values[sources]
    gate_own = gates[sources]
    cot_own = cotangent[sources]
    ends = jnp.cumsum(lengths)
    rim = (WIN_BLK - 1) * BLOCK
    key_ext = jnp.concatenate([jnp.zeros((rim, D), key_own.dtype), key_own], axis=0)
    value_ext = jnp.concatenate([jnp.zeros((rim, D), value_own.dtype), value_own], axis=0)
    flags = pattern.astype(jnp.float32)
    stride = 16
    turns = N_BLK // stride

    def piece(index):
        first = index * stride
        starts = (first + jnp.arange(stride, dtype=jnp.int32)) * BLOCK
        query_blocks = lax.dynamic_slice_in_dim(query_own, first * BLOCK, stride * BLOCK, 0).reshape(stride, BLOCK, D)
        key_part = lax.dynamic_slice_in_dim(key_ext, first * BLOCK, (stride + WIN_BLK - 1) * BLOCK, 0)
        value_part = lax.dynamic_slice_in_dim(value_ext, first * BLOCK, (stride + WIN_BLK - 1) * BLOCK, 0)
        mask = window_mask(starts, lax.dynamic_slice_in_dim(flags, first, stride, 0), ends, EVENTS, BLOCK, WIN_BLK)
        return (query_blocks, windows(key_part, stride, BLOCK, WIN_BLK), windows(value_part, stride, BLOCK, WIN_BLK), mask)

    def forward_step(index):
        query_blocks, key_win, value_win, mask = piece(index)
        return attend_forward(query_blocks, key_win, value_win, mask, bias_full)[2]
    outputs = lax.map(forward_step, jnp.arange(turns, dtype=jnp.int32)).reshape(EVENTS, D)
    normed, inverse = norm_parts(outputs)
    gate_grad = (cot_own.astype(jnp.float32) * normed).astype(jnp.bfloat16)
    grad_normed = cot_own.astype(jnp.float32) * gate_own.astype(jnp.float32)
    grad_out = norm_back(grad_normed, normed, inverse).astype(jnp.bfloat16)

    def backward_step(carry, index):
        key_acc, value_acc, bias_acc = carry
        query_blocks, key_win, value_win, mask = piece(index)
        scores, weights, _ = attend_forward(query_blocks, key_win, value_win, mask, bias_full)
        first = index * stride
        grad_blocks = lax.dynamic_slice_in_dim(grad_out, first * BLOCK, stride * BLOCK, 0).reshape(stride, BLOCK, D)
        grad_scores, query_grad, key_terms, value_terms = attend_backward(query_blocks, key_win, value_win, mask, scores, weights, grad_blocks, HEADS)
        span_rows = (stride + WIN_BLK - 1) * BLOCK
        cur_key = lax.dynamic_slice_in_dim(key_acc, first * BLOCK, span_rows, 0)
        key_acc = lax.dynamic_update_slice_in_dim(key_acc, cur_key + fold_window(key_terms), first * BLOCK, 0)
        cur_value = lax.dynamic_slice_in_dim(value_acc, first * BLOCK, span_rows, 0)
        value_acc = lax.dynamic_update_slice_in_dim(value_acc, cur_value + fold_window(value_terms), first * BLOCK, 0)
        bias_acc = bias_acc + grad_scores.sum(0).reshape(HEADS, -1)
        return ((key_acc, value_acc, bias_acc), query_grad.astype(jnp.bfloat16))
    start_carry = (jnp.zeros((EVENTS + rim, D), jnp.float32), jnp.zeros((EVENTS + rim, D), jnp.float32), jnp.zeros((HEADS, BLOCK * WIN_BLK * BLOCK), jnp.float32))
    (key_acc, value_acc, bias_acc), query_grads = lax.scan(backward_step, start_carry, jnp.arange(turns, dtype=jnp.int32))
    query_grad = query_grads.reshape(EVENTS, D)
    key_grad = key_acc[rim:].astype(jnp.bfloat16)
    value_grad = value_acc[rim:].astype(jnp.bfloat16)
    bias_part = jnp.einsum('hp,kp->hk', bias_acc, onehot, precision=HIGH)

    def back_home(rows_own):
        return jnp.zeros((EVENTS, D), rows_own.dtype).at[sources].set(rows_own)
    return (back_home(query_grad), back_home(key_grad), back_home(value_grad), back_home(gate_grad), bias_part)

def reference(queries, keys, values, gates, cotangent, rel_bias, lengths, send_counts, block_pattern):
    bias_full, onehot = bias_table(rel_bias, BLOCK, WIN_BLK)
    query_grad, key_grad, value_grad, gate_grad, bias_parts = lax.map(lambda arrays: group_pass(arrays, bias_full, onehot), (queries, keys, values, gates, cotangent, lengths, send_counts, block_pattern))
    bias_grad = lax.optimization_barrier(jnp.sum(bias_parts, axis=0)) / math.sqrt(GROUPS * EVENTS)
    return (query_grad, key_grad, value_grad, gate_grad, bias_grad)
```

```python
import math

import jax
import jax.numpy as jnp
from jax import lax
from jax.experimental import pallas as pl
from jax.experimental.pallas import tpu as pltpu
from jax.sharding import PartitionSpec as P

MESH = pl.DeviceIdType.MESH
F32 = jnp.float32
BF16 = jnp.bfloat16

NX, NZ, NY, NC = 4, 8, 2, 2
PEERS = NX * NZ * NY * NC
BATCH = 4
ROWS = 256
WIDTH = 1024
HEADS = 8
SIZE = 128
CHUNKS = WIDTH // 128
BLOCK = 128
SPAN = 256
BUCKETS = 32
SLOTS = 3
EPS = 1e-05
SCALE = SIZE ** (-0.5)


def coords(me):
    return me // (NZ * NY * NC), (me // (NY * NC)) % NZ, (me // NC) % NY, me % NC


def place(x, z, y, c):
    return ((x * NZ + z) * NY + y) * NC + c


def partner(me, k, sign=1):
    x, z, y, c = coords(me)
    dx, dz, dy, dc = coords(k)
    if sign < 0:
        dx, dz = NX - dx, NZ - dz
    return place((x + dx) % NX, (z + dz) % NZ, (y + dy) % NY, (c + dc) % NC)


def stage(dst, pick, value_of):
    for c in range(CHUNKS):
        rows = matmul(pick, value_of(slice(c * 128, (c + 1) * 128)), 1, 0)
        dst[pl.ds(c, PEERS * SLOTS, stride=CHUNKS), :] = rows


def unstage(src, pick, write):
    for c in range(CHUNKS):
        rows = src[pl.ds(c, PEERS * SLOTS, stride=CHUNKS), :].astype(BF16)
        write(slice(c * 128, (c + 1) * 128), matmul(pick, rows, 1, 0))


def pack(dst, at, first, second):
    for s in range(SLOTS):
        off = pl.multiple_of((at * SLOTS + s) * CHUNKS, CHUNKS)
        tile = jnp.concatenate([first[pl.ds(off, CHUNKS), :], second[pl.ds(off, CHUNKS), :]], axis=0)
        dst[at * SLOTS + s] = tile.astype(BF16)


def unpack(recv, first, second):
    step = 8

    def some(i, carry):
        for j in range(step):
            p = i * step + j
            tile = recv[p].astype(F32)
            off = pl.multiple_of(p * CHUNKS, CHUNKS)
            first[pl.ds(off, CHUNKS), :] = tile[:CHUNKS]
            second[pl.ds(off, CHUNKS), :] = tile[CHUNKS:]
        return carry

    lax.fori_loop(0, PEERS * SLOTS // step, some, 0)


def ones_where(index, axis):
    shape = (ROWS, PEERS * SLOTS) if axis == 0 else (PEERS * SLOTS, ROWS)
    return jnp.where(lax.broadcasted_iota(jnp.int32, shape, axis) == index, 1.0, 0.0).astype(BF16)


def wait_bytes(ref, sem):
    pltpu.make_async_copy(ref, ref, sem).wait()


def matmul(a, b, ca, cb):
    return lax.dot_general(a, b, (((ca,), (cb,)), ((), ())), preferred_element_type=F32)


def kernel(
    q_in, k_in, v_in, g_in, c_in, rel, lengths, pattern, out_col, out_row, in_col, in_row,
    gq_out, gk_out, gv_out, gg_out, bias_out,
    send, recv_0, recv_1, recv_2, recv_3, stage_a, stage_b, q_own, k_ext, v_ext, gn_own, a_all, d_all, table, mask,
    o_all, go_all, gq_acc, gk_acc, gv_acc, halo_out, halo_in, gs_sum, part, red, cur,
    send_sem, recv_sem, halo_send, halo_recv, red_send, red_recv,
):
    recv = (recv_0, recv_1, recv_2, recv_3)
    me = lax.axis_index("ctx")
    grp = lax.axis_index("batch")
    x, z, y, c = coords(me)

    def ctx(i):
        return {"device_id": (grp, i), "device_id_type": MESH}

    barrier = pltpu.get_barrier_semaphore()

    def greet(k, carry):
        pl.semaphore_signal(barrier, inc=1, **ctx(partner(me, k)))
        return carry

    lax.fori_loop(1, PEERS, greet, 0)
    for d in range(1, BATCH):
        pl.semaphore_signal(barrier, inc=1, device_id=((grp + d) % BATCH, me), device_id_type=MESH)

    def exchange(group, first, second):
        out, into = send.at[group], recv[group]

        def one(k, carry):
            to = partner(me, k)
            pack(out, k, first, second)
            pltpu.make_async_remote_copy(
                src_ref=out.at[pl.ds(k * SLOTS, SLOTS)],
                dst_ref=into.at[pl.ds(k * SLOTS, SLOTS)],
                send_sem=send_sem.at[group],
                recv_sem=recv_sem.at[group],
                **ctx(to),
            ).start()
            return carry

        lax.fori_loop(1, PEERS, one, 0)
        pack(into, 0, first, second)

    def arrived(group):
        wait_bytes(recv[group].at[pl.ds(SLOTS, (PEERS - 1) * SLOTS)], recv_sem.at[group])

    def halo_copy(i, src, dst, to):
        return pltpu.make_async_remote_copy(
            src_ref=src, dst_ref=dst, send_sem=halo_send.at[i], recv_sem=halo_recv.at[i], **ctx(to)
        )

    pick = ones_where(out_col[...], 1)
    stage(stage_a, pick, lambda f: q_in[:, f])
    stage(stage_b, pick, lambda f: k_in[:, f])
    pl.semaphore_wait(barrier, PEERS - 1 + BATCH - 1)
    exchange(0, stage_a, stage_b)
    stage(stage_a, pick, lambda f: v_in[:, f])
    stage(stage_b, pick, lambda f: (c_in[:, f].astype(F32) * g_in[:, f].astype(F32)).astype(BF16))
    exchange(1, stage_a, stage_b)

    row_i = lax.broadcasted_iota(jnp.int32, (BLOCK, SPAN), 0)
    col_c = lax.broadcasted_iota(jnp.int32, (BLOCK, SPAN), 1)
    bucket = (row_i + BLOCK - col_c) >> 3

    def bias_of(h, carry):
        full = jnp.zeros((BLOCK, SPAN), F32)
        for k in range(BUCKETS):
            full = jnp.where(bucket == k, rel[h, k], full)
        table[h] = full
        return carry

    lax.fori_loop(0, HEADS, bias_of, 0)
    for b in range(2):
        pos_q = me * ROWS + b * BLOCK + row_i
        pos_k = me * ROWS + (b - 1) * BLOCK + col_c
        hist_q = jnp.zeros((BLOCK, SPAN), jnp.int32)
        hist_k = jnp.zeros((BLOCK, SPAN), jnp.int32)
        end = jnp.int32(0)
        for i in range(lengths.shape[0]):
            end = end + lengths[i]
            hist_q = hist_q + (pos_q >= end).astype(jnp.int32)
            hist_k = hist_k + (pos_k >= end).astype(jnp.int32)
        flag = jnp.where(col_c >= BLOCK, pattern[2 * b], pattern[2 * b + 1])
        live = (pos_k <= pos_q) & (pos_k >= 0) & (hist_q == hist_k) & (flag > 0)
        mask[b] = jnp.where(live, 1.0 / SPAN, 0.0).astype(F32)

    arrived(0)
    settle = ones_where(in_row[...], 0)
    unpack(recv[0], stage_a, stage_b)

    def put_q(f, v):
        q_own[:, f] = v.astype(BF16)

    def put_k(f, v):
        k_ext[BLOCK:, f] = v.astype(BF16)

    def put_v(f, v):
        v_ext[BLOCK:, f] = v.astype(BF16)

    def put_gn(f, v):
        gn_own[:, f] = v

    after, before = (me + 1) % PEERS, (me + PEERS - 1) % PEERS
    unstage(stage_b, settle, put_k)
    k_halo = halo_copy(0, k_ext.at[pl.ds(ROWS, BLOCK)], k_ext.at[pl.ds(0, BLOCK)], after)
    k_halo.start()
    unstage(stage_a, settle, put_q)

    def score(b):
        def one(h, carry):
            f = pl.ds(pl.multiple_of(h * SIZE, SIZE), SIZE)
            raw = matmul(q_own[pl.ds(b * BLOCK, BLOCK), f], k_ext[pl.ds(b * BLOCK, SPAN), f], 1, 1)
            s = raw * SCALE + table[h]
            sig = jax.nn.sigmoid(s)
            m = mask[b]
            a_all[b, h] = (s * sig * m).astype(BF16)
            d_all[b, h] = sig * (1.0 + s * (1.0 - sig)) * m
            return carry

        lax.fori_loop(0, HEADS, one, 0)

    score(1)
    k_halo.wait_recv()
    score(0)

    arrived(1)
    unpack(recv[1], stage_a, stage_b)
    unstage(stage_a, settle, put_v)
    v_halo = halo_copy(1, v_ext.at[pl.ds(ROWS, BLOCK)], v_ext.at[pl.ds(0, BLOCK)], after)
    v_halo.start()
    unstage(stage_b, settle, put_gn)

    def output(b):
        def one(h, carry):
            f = pl.ds(pl.multiple_of(h * SIZE, SIZE), SIZE)
            o_all[pl.ds(b * BLOCK, BLOCK), f] = matmul(a_all[b, h], v_ext[pl.ds(b * BLOCK, SPAN), f], 1, 0)
            return carry

        lax.fori_loop(0, HEADS, one, 0)

    output(1)
    v_halo.wait_recv()
    output(0)

    def norm(i, carry):
        rows = pl.ds(pl.multiple_of(i * 32, 32), 32)
        out = o_all[rows, :]
        center = out - jnp.mean(out, axis=-1, keepdims=True)
        inverse = lax.rsqrt(jnp.mean(center * center, axis=-1, keepdims=True) + EPS)
        normed = center * inverse
        gn = gn_own[rows, :]
        go = (
            gn
            - jnp.mean(gn, axis=-1, keepdims=True)
            - normed * jnp.mean(gn * normed, axis=-1, keepdims=True)
        ) * inverse
        o_all[rows, :] = normed
        go_all[rows, :] = go.astype(BF16)
        return carry

    lax.fori_loop(0, ROWS // 32, norm, 0)

    def back(b):
        def one(h, carry):
            f = pl.ds(pl.multiple_of(h * SIZE, SIZE), SIZE)
            own = pl.ds(b * BLOCK, BLOCK)
            win = pl.ds(b * BLOCK, SPAN)
            go = go_all[own, f]
            gs = matmul(go, v_ext[win, f], 1, 1) * d_all[b, h]
            low = gs.astype(BF16)
            gq_acc[own, f] = matmul(low, k_ext[win, f], 1, 0) * SCALE
            gk = matmul(low, q_own[own, f], 0, 0) * SCALE
            gv = matmul(a_all[b, h], go, 0, 0)
            if b == 0:
                gs_sum[h] = gs
                halo_out[0, :, f] = gk[:BLOCK].astype(BF16)
                halo_out[1, :, f] = gv[:BLOCK].astype(BF16)
                gk_acc[pl.ds(0, BLOCK), f] = gk[BLOCK:]
                gv_acc[pl.ds(0, BLOCK), f] = gv[BLOCK:]
            else:
                gs_sum[h] += gs
                gk_acc[pl.ds(0, BLOCK), f] += gk[:BLOCK]
                gv_acc[pl.ds(0, BLOCK), f] += gv[:BLOCK]
                gk_acc[pl.ds(BLOCK, BLOCK), f] = gk[BLOCK:]
                gv_acc[pl.ds(BLOCK, BLOCK), f] = gv[BLOCK:]
            return carry

        lax.fori_loop(0, HEADS, one, 0)

    back(0)
    g_halo = halo_copy(2, halo_out, halo_in, before)
    g_halo.start()
    back(1)

    pick = ones_where(in_col[...], 1)
    stage(stage_a, pick, lambda f: o_all[:, f].astype(BF16))
    stage(stage_b, pick, lambda f: gq_acc[:, f].astype(BF16))
    exchange(2, stage_a, stage_b)

    def buckets_of(h, carry):
        gs = gs_sum[h]
        for k in range(BUCKETS):
            picked = jnp.where(bucket == k, gs, 0.0)
            part[pl.ds(h * BUCKETS + k, 1), :] = jnp.sum(picked, axis=0, keepdims=True)
        return carry

    lax.fori_loop(0, HEADS, buckets_of, 0)
    sums = jnp.sum(part[...], axis=1, keepdims=True)
    eye = lax.broadcasted_iota(jnp.int32, (128, 128), 0) == lax.broadcasted_iota(jnp.int32, (128, 128), 1)
    lines = [
        jnp.sum(jnp.where(eye, sums[r * 128 : (r + 1) * 128], 0.0), axis=0, keepdims=True) for r in range(2)
    ]
    first_total = jnp.concatenate(lines + [jnp.zeros((6, 128), F32)], axis=0)

    rounds = (
        (NY * NC, y * NC + c, lambda i: (grp, place(x, z, i // NC, i % NC))),
        (NZ, z, lambda i: (grp, place(x, i, y, c))),
        (NX, x, lambda i: (grp, place(i, z, y, c))),
        (BATCH, grp, lambda i: (i, me)),
    )

    def round_start(r, value):
        n, mine, device = rounds[r]
        cur[r] = value
        red[r, mine] = value
        for d in range(1, n):
            pltpu.make_async_remote_copy(
                src_ref=cur.at[r],
                dst_ref=red.at[r, mine],
                send_sem=red_send.at[r],
                recv_sem=red_recv.at[r],
                device_id=device((mine + d) % n),
                device_id_type=MESH,
            ).start()

    def round_end(r):
        n = rounds[r][0]
        wait_bytes(red.at[r, pl.ds(0, n - 1)], red_recv.at[r])
        total = red[r, 0]
        for i in range(1, n):
            total = total + red[r, i]
        return total

    round_start(0, first_total)

    g_halo.wait_recv()
    for acc, i in ((gk_acc, 0), (gv_acc, 1)):
        acc[BLOCK:, :] = acc[BLOCK:, :] + halo_in[i].astype(F32)
    stage(stage_a, pick, lambda f: gk_acc[:, f].astype(BF16))
    stage(stage_b, pick, lambda f: gv_acc[:, f].astype(BF16))
    exchange(3, stage_a, stage_b)

    round_start(1, round_end(0))
    round_start(2, round_end(1))
    arrived(2)
    land = ones_where(out_row[...], 0)
    unpack(recv[2], stage_a, stage_b)

    def put_gate(f, v):
        gg_out[:, f] = (c_in[:, f].astype(F32) * v).astype(BF16)

    def put_gq(f, v):
        gq_out[:, f] = v.astype(BF16)

    def put_gk(f, v):
        gk_out[:, f] = v.astype(BF16)

    def put_gv(f, v):
        gv_out[:, f] = v.astype(BF16)

    unstage(stage_a, land, put_gate)
    unstage(stage_b, land, put_gq)
    round_start(3, round_end(2))
    bias_out[...] = round_end(3) * (1.0 / math.sqrt(BATCH * PEERS * ROWS))

    arrived(3)
    unpack(recv[3], stage_a, stage_b)
    unstage(stage_a, land, put_gk)
    unstage(stage_b, land, put_gv)

    for group in range(4):
        wait_bytes(send.at[group, pl.ds(SLOTS, (PEERS - 1) * SLOTS)], send_sem.at[group])
    k_halo.wait_send()
    v_halo.wait_send()
    g_halo.wait_send()
    for r in range(4):
        wait_bytes(red.at[r, pl.ds(0, rounds[r][0] - 1)], red_send.at[r])


def slots_of(counts, me):
    ids = jnp.arange(PEERS, dtype=jnp.int32)
    first = jnp.sum(jnp.where(ids[None, :] < ids[:, None], counts[None, :], 0), axis=1)
    slot = jnp.arange(SLOTS, dtype=jnp.int32)

    def ordered(sign):
        other = partner(me, ids, sign)[:, None] == ids[None, :]
        start = jnp.sum(jnp.where(other, first[None, :], 0), axis=1)
        count = jnp.sum(jnp.where(other, counts[None, :], 0), axis=1)
        rows = jnp.where(slot[None, :] < count[:, None], start[:, None] + slot[None, :], -1)
        return rows.reshape(-1)

    return ordered(1)[:, None], ordered(-1)[None, :]


def body(queries, keys, values, gates, cotangent, rel_bias, lengths, send_counts, block_pattern):
    me = lax.axis_index("ctx")
    counts = send_counts[0]
    out_col, out_row = slots_of(lax.dynamic_index_in_dim(counts, me, 0, keepdims=False), me)
    in_col, in_row = slots_of(lax.dynamic_index_in_dim(counts, me, 1, keepdims=False), me)
    vmem = pl.BlockSpec(memory_space=pltpu.VMEM)
    smem = pl.BlockSpec(memory_space=pltpu.SMEM)
    event = jax.ShapeDtypeStruct((ROWS, WIDTH), BF16)
    buffer = (PEERS * SLOTS, 16, 128)
    gq, gk, gv, gg, bias = pl.pallas_call(
        kernel,
        out_shape=(event, event, event, event, jax.ShapeDtypeStruct((8, 128), F32)),
        in_specs=[vmem] * 5 + [smem] * 3 + [vmem] * 4,
        out_specs=(vmem,) * 5,
        scratch_shapes=[
            pltpu.VMEM((4,) + buffer, BF16),
            pltpu.VMEM(buffer, BF16),
            pltpu.VMEM(buffer, BF16),
            pltpu.VMEM(buffer, BF16),
            pltpu.VMEM(buffer, BF16),
            pltpu.VMEM((PEERS * SLOTS * CHUNKS, 128), F32),
            pltpu.VMEM((PEERS * SLOTS * CHUNKS, 128), F32),
            pltpu.VMEM((ROWS, WIDTH), BF16),
            pltpu.VMEM((ROWS + BLOCK, WIDTH), BF16),
            pltpu.VMEM((ROWS + BLOCK, WIDTH), BF16),
            pltpu.VMEM((ROWS, WIDTH), F32),
            pltpu.VMEM((2, HEADS, BLOCK, SPAN), BF16),
            pltpu.VMEM((2, HEADS, BLOCK, SPAN), F32),
            pltpu.VMEM((HEADS, BLOCK, SPAN), F32),
            pltpu.VMEM((2, BLOCK, SPAN), F32),
            pltpu.VMEM((ROWS, WIDTH), F32),
            pltpu.VMEM((ROWS, WIDTH), BF16),
            pltpu.VMEM((ROWS, WIDTH), F32),
            pltpu.VMEM((ROWS, WIDTH), F32),
            pltpu.VMEM((ROWS, WIDTH), F32),
            pltpu.VMEM((2, BLOCK, WIDTH), BF16),
            pltpu.VMEM((2, BLOCK, WIDTH), BF16),
            pltpu.VMEM((HEADS, BLOCK, SPAN), F32),
            pltpu.VMEM((HEADS * BUCKETS, SPAN), F32),
            pltpu.VMEM((4, 8, 8, 128), F32),
            pltpu.VMEM((4, 8, 128), F32),
            pltpu.SemaphoreType.DMA((4,)),
            pltpu.SemaphoreType.DMA((4,)),
            pltpu.SemaphoreType.DMA((3,)),
            pltpu.SemaphoreType.DMA((3,)),
            pltpu.SemaphoreType.DMA((4,)),
            pltpu.SemaphoreType.DMA((4,)),
        ],
        compiler_params=pltpu.CompilerParams(
            collective_id=0, has_side_effects=True, vmem_limit_bytes=56 * 1024 * 1024
        ),
    )(
        queries[0], keys[0], values[0], gates[0], cotangent[0],
        rel_bias, lengths[0], block_pattern[0].reshape(-1),
        out_col, out_row, in_col, in_row,
    )
    return gq[None], gk[None], gv[None], gg[None], bias[:2].reshape(HEADS, BUCKETS)


def solution(mesh):
    event = P("batch", "ctx", None)
    return jax.shard_map(
        body,
        mesh=mesh,
        in_specs=(event,) * 5 + (P(), P("batch", None), P("batch", None, None), event),
        out_specs=(event,) * 4 + (P(),),
        check_vma=False,
    )
```

```python
import math

import jax
import jax.numpy as jnp
from jax import lax
from jax.experimental import pallas as pl
from jax.experimental.pallas import tpu as pltpu
from jax.sharding import PartitionSpec as P

MESH = pl.DeviceIdType.MESH
F32 = jnp.float32
BF16 = jnp.bfloat16

NX, NZ, NY, NC = 4, 8, 2, 2
PEERS = NX * NZ * NY * NC
BATCH = 4
ROWS = 256
WIDTH = 1024
HEADS = 8
SIZE = 128
CHUNKS = WIDTH // 128
BLOCK = 128
SPAN = 256
BUCKETS = 32
SLOTS = 3
EPS = 1e-05
LINES = PEERS * SLOTS
STEP = 16
SCALE = SIZE ** (-0.5)


def coords(me):
    return me // (NZ * NY * NC), (me // (NY * NC)) % NZ, (me // NC) % NY, me % NC


def place(x, z, y, c):
    return ((x * NZ + z) * NY + y) * NC + c


def partner(me, k):
    x, z, y, c = coords(me)
    dx, dz, dy, dc = coords(k)
    return place((x + dx) % NX, (z + dz) % NZ, (y + dy) % NY, (c + dc) % NC)


def partners_of(me, k, sign):
    x, z, y, c = coords(me)
    dx, dz, dy, dc = k >> 5, (k >> 2) & 7, (k >> 1) & 1, k & 1
    return place((x + sign * dx) & 3, (z + sign * dz) & 7, (y + dy) & 1, (c + dc) & 1)


def eye_turn(vector):
    eye = lax.broadcasted_iota(jnp.int32, (128, 128), 0) == lax.broadcasted_iota(jnp.int32, (128, 128), 1)
    return jnp.sum(jnp.where(eye, vector, 0.0), axis=1 if vector.shape[0] == 1 else 0, keepdims=True)


def travel(me, row, col, axis, sign):
    shape = (LINES, 128) if axis == 0 else (128, LINES)
    device = lax.broadcasted_iota(jnp.int32, shape, 1 - axis)
    along = lax.broadcasted_iota(jnp.int32, shape, axis)
    k = (along * 171) >> 9
    same = partners_of(me, k, sign) == device
    pairs = (128, 128)
    below = lax.broadcasted_iota(jnp.int32, pairs, 1 - axis) < lax.broadcasted_iota(jnp.int32, pairs, axis)
    counts = row if axis == 0 else col
    lower = jnp.sum(jnp.where(below, counts, 0.0), axis=1 - axis, keepdims=True)
    lower = eye_turn(lower)
    count = jnp.sum(jnp.where(same, counts, 0.0), axis=1 - axis, keepdims=True)
    start = jnp.sum(jnp.where(same, lower, 0.0), axis=1 - axis, keepdims=True)
    line = lax.broadcasted_iota(jnp.int32, count.shape, axis)
    slot = (line - ((line * 171) >> 9) * SLOTS).astype(F32)
    index = jnp.where(slot < count, start + slot, -1.0)
    full = (LINES, ROWS) if axis == 0 else (ROWS, LINES)
    rows = lax.broadcasted_iota(jnp.int32, full, 1 - axis).astype(F32)
    return jnp.where(rows == index, 1.0, 0.0).astype(BF16)


def unstage(src, pick, write):
    for c in range(CHUNKS):
        rows = src[pl.ds(c, LINES, stride=CHUNKS), :].astype(BF16)
        write(slice(c * 128, (c + 1) * 128), matmul(pick[...], rows, 1, 0))


def unpack(recv, tiles):
    step = 4

    def some(i, carry):
        for j in range(step):
            k = i * step + j
            for t, halves in enumerate(tiles):
                tile = recv[k * len(tiles) + t].astype(F32)
                for h, (buffer, slot) in enumerate(halves):
                    off = pl.multiple_of((k * SLOTS + slot) * CHUNKS, CHUNKS)
                    buffer[pl.ds(off, CHUNKS), :] = tile[h * CHUNKS : (h + 1) * CHUNKS]
        return carry

    lax.fori_loop(0, PEERS // step, some, 0)


def wait_bytes(ref, sem):
    pltpu.make_async_copy(ref, ref, sem).wait()


def matmul(a, b, ca, cb):
    return lax.dot_general(a, b, (((ca,), (cb,)), ((), ())), preferred_element_type=F32)


def kernel(
    q_in, k_in, v_in, g_in, c_in, rel, lengths, pattern, counts,
    gq_out, gk_out, gv_out, gg_out, bias_out,
    send_0, send_1, send_2, send_3, send_4, send_5, recv_0, recv_1, recv_2, recv_3, recv_4, recv_5,
    stage_a, stage_b, send_out, send_in, settle, land, gn_low, n_low, gq_low, gk_low, gv_low,
    q_own, k_ext, v_ext, gn_own, inv, a_all, d_all, table, mask,
    o_all, go_all, gk_acc, gv_acc, halo_out, halo_in, gs_sum, part, red, cur,
    send_sem, recv_sem, halo_send, halo_recv, red_send, red_recv, ready,
):
    send = (send_0, send_1, send_2, send_3, send_4, send_5)
    recv = (recv_0, recv_1, recv_2, recv_3, recv_4, recv_5)
    me = lax.axis_index("ctx")
    grp = lax.axis_index("batch")
    x, z, y, c = coords(me)

    def ctx(i):
        return {"device_id": (grp, i), "device_id_type": MESH}

    barrier = pltpu.get_barrier_semaphore()
    line = [place(x, (z + d) % NZ, y, c) for d in range(1, NZ)]
    plane = [
        place((x + dx) % NX, z, (y + dy) % NY, (c + dc) % NC)
        for dx in range(NX) for dy in range(NY) for dc in range(NC)
    ][1:]
    for to in line + plane:
        pl.semaphore_signal(barrier, inc=1, **ctx(to))
    for d in range(1, BATCH):
        pl.semaphore_signal(barrier, inc=1, device_id=((grp + d) % BATCH, me), device_id_type=MESH)

    def exchange(group, tiles, staged, pick):
        out, into, n = send[group], recv[group], len(tiles)

        def pack(dst, k):
            for t, halves in enumerate(tiles):
                pieces = []
                for buffer, slot in halves:
                    off = pl.multiple_of((k * SLOTS + slot) * CHUNKS, CHUNKS)
                    pieces.append(buffer[pl.ds(off, CHUNKS), :])
                dst[k * n + t] = jnp.concatenate(pieces, axis=0).astype(BF16)

        def one(k, carry):
            pack(out, k)
            pltpu.make_async_remote_copy(
                src_ref=out.at[pl.ds(k * n, n)],
                dst_ref=into.at[pl.ds(k * n, n)],
                send_sem=send_sem.at[group],
                recv_sem=recv_sem.at[group],
                **ctx(partner(me, k)),
            ).start()
            return carry

        def stage(i):
            for buffer, value in staged:
                lines = pl.ds(pl.multiple_of(i * STEP * SLOTS, STEP * SLOTS), STEP * SLOTS)
                rows = matmul(pick[lines, :], value[...], 1, 0)
                for f in range(CHUNKS):
                    to = pl.ds(i * STEP * SLOTS * CHUNKS + f, STEP * SLOTS, stride=CHUNKS)
                    buffer[to, :] = rows[:, f * 128 : (f + 1) * 128]

        def chunk(i, carry):
            stage(i)
            return lax.fori_loop(i * STEP, i * STEP + STEP, one, carry)

        stage(0)
        lax.fori_loop(1, STEP, one, 0)
        pack(into, 0)
        lax.fori_loop(1, PEERS // STEP, chunk, 0)

    def arrived(group):
        n = recv[group].shape[0] // PEERS
        wait_bytes(recv[group].at[pl.ds(n, (PEERS - 1) * n)], recv_sem.at[group])

    def halo_copy(i, src, dst, to):
        return pltpu.make_async_remote_copy(
            src_ref=src, dst_ref=dst, send_sem=halo_send.at[i], recv_sem=halo_recv.at[i], **ctx(to)
        )

    out_row = counts[pl.ds(me, 1), :].astype(F32)
    lane = lax.broadcasted_iota(jnp.int32, (PEERS, PEERS), 1)
    in_col = jnp.sum(jnp.where(lane == me, counts[...].astype(F32), 0.0), axis=1, keepdims=True)
    out_col, in_row = eye_turn(out_row), eye_turn(in_col)
    send_out[...] = travel(me, out_row, out_col, 0, 1)

    gn_low[...] = (c_in[...].astype(F32) * g_in[...].astype(F32)).astype(BF16)
    pl.semaphore_wait(barrier, len(line) + len(plane) + BATCH - 1)
    for to in line:
        pl.semaphore_signal(ready, inc=1, **ctx(to))
    pl.semaphore_wait(ready, len(line))
    by_two = lambda a, b: (((a, 0), (b, 0)), ((a, 1), (b, 1)), ((a, 2), (b, 2)))
    exchange(0, by_two(stage_a, stage_b), ((stage_a, k_in), (stage_b, v_in)), send_out)
    rest = ((stage_b, 1), (stage_b, 2)),
    full = ((stage_a, 0), (stage_a, 1)), ((stage_a, 2), (stage_b, 0))
    exchange(1, full, ((stage_a, q_in), (stage_b, gn_low)), send_out)
    exchange(2, rest, (), send_out)
    settle[...] = travel(me, in_row, in_col, 1, -1)

    row_i = lax.broadcasted_iota(jnp.int32, (BLOCK, SPAN), 0)
    col_c = lax.broadcasted_iota(jnp.int32, (BLOCK, SPAN), 1)
    bucket = (row_i + BLOCK - col_c) >> 3

    def bias_of(h, carry):
        full = jnp.zeros((BLOCK, SPAN), F32)
        for k in range(BUCKETS):
            full = jnp.where(bucket == k, rel[h, k], full)
        table[h] = full
        return carry

    lax.fori_loop(0, HEADS, bias_of, 0)
    for b in range(2):
        pos_q = me * ROWS + b * BLOCK + row_i
        pos_k = me * ROWS + (b - 1) * BLOCK + col_c
        hist_q = jnp.zeros((BLOCK, SPAN), jnp.int32)
        hist_k = jnp.zeros((BLOCK, SPAN), jnp.int32)
        end = jnp.int32(0)
        for i in range(lengths.shape[1]):
            end = end + lengths[0, i]
            hist_q = hist_q + (pos_q >= end).astype(jnp.int32)
            hist_k = hist_k + (pos_k >= end).astype(jnp.int32)
        flag = jnp.where(col_c >= BLOCK, pattern[0, b, 0], pattern[0, b, 1])
        live = (pos_k <= pos_q) & (pos_k >= 0) & (hist_q == hist_k) & (flag > 0)
        mask[b] = jnp.where(live, 1.0 / SPAN, 0.0).astype(F32)

    def put_q(f, v):
        q_own[:, f] = v.astype(BF16)

    def put_k(f, v):
        k_ext[BLOCK:, f] = v.astype(BF16)

    def put_v(f, v):
        v_ext[BLOCK:, f] = v.astype(BF16)

    def put_gn(f, v):
        gn_own[:, f] = v

    after, before = (me + 1) % PEERS, (me + PEERS - 1) % PEERS
    arrived(0)
    unpack(recv[0], by_two(stage_a, stage_b))
    unstage(stage_a, settle, put_k)
    k_halo = halo_copy(0, k_ext.at[pl.ds(ROWS, BLOCK)], k_ext.at[pl.ds(0, BLOCK)], after)
    k_halo.start()
    unstage(stage_b, settle, put_v)
    v_halo = halo_copy(1, v_ext.at[pl.ds(ROWS, BLOCK)], v_ext.at[pl.ds(0, BLOCK)], after)
    v_halo.start()
    send_in[...] = travel(me, in_row, in_col, 0, 1)
    land[...] = travel(me, out_row, out_col, 1, -1)

    def forward(b):
        def one(h, carry):
            f = pl.ds(pl.multiple_of(h * SIZE, SIZE), SIZE)
            raw = matmul(q_own[pl.ds(b * BLOCK, BLOCK), f], k_ext[pl.ds(b * BLOCK, SPAN), f], 1, 1)
            s = raw * SCALE + table[h]
            sig = jax.nn.sigmoid(s)
            m = mask[b]
            a = (s * sig * m).astype(BF16)
            a_all[b, h] = a
            d_all[b, h] = sig * (1.0 + s * (1.0 - sig)) * m
            o_all[pl.ds(b * BLOCK, BLOCK), f] = matmul(a, v_ext[pl.ds(b * BLOCK, SPAN), f], 1, 0)
            return carry

        lax.fori_loop(0, HEADS, one, 0)

    arrived(1)
    unpack(recv[1], full)
    unstage(stage_a, settle, put_q)
    forward(1)
    k_halo.wait_recv()
    v_halo.wait_recv()
    forward(0)

    def norm(i, carry):
        rows = pl.ds(pl.multiple_of(i * 32, 32), 32)
        out = o_all[rows, :]
        center = out - jnp.mean(out, axis=-1, keepdims=True)
        inverse = lax.rsqrt(jnp.mean(center * center, axis=-1, keepdims=True) + EPS)
        normed = center * inverse
        o_all[rows, :] = normed
        n_low[rows, :] = normed.astype(BF16)
        inv[rows, :] = jnp.broadcast_to(inverse, (32, 128))
        return carry

    lax.fori_loop(0, ROWS // 32, norm, 0)
    exchange(3, (((stage_a, 0), (stage_a, 1)),), ((stage_a, n_low),), send_in)

    arrived(2)
    unpack(recv[2], rest)
    unstage(stage_b, settle, put_gn)

    def norm_back(i, carry):
        rows = pl.ds(pl.multiple_of(i * 32, 32), 32)
        normed = o_all[rows, :]
        gn = gn_own[rows, :]
        go = (
            gn
            - jnp.mean(gn, axis=-1, keepdims=True)
            - normed * jnp.mean(gn * normed, axis=-1, keepdims=True)
        ) * inv[rows, :1]
        go_all[rows, :] = go.astype(BF16)
        return carry

    lax.fori_loop(0, ROWS // 32, norm_back, 0)

    def back(b):
        def one(h, carry):
            f = pl.ds(pl.multiple_of(h * SIZE, SIZE), SIZE)
            own = pl.ds(b * BLOCK, BLOCK)
            win = pl.ds(b * BLOCK, SPAN)
            go = go_all[own, f]
            gs = matmul(go, v_ext[win, f], 1, 1) * d_all[b, h]
            low = gs.astype(BF16)
            gq_low[own, f] = (matmul(low, k_ext[win, f], 1, 0) * SCALE).astype(BF16)
            gk = matmul(low, q_own[own, f], 0, 0) * SCALE
            gv = matmul(a_all[b, h], go, 0, 0)
            if b == 0:
                gs_sum[h] = gs
                halo_out[0, :, f] = gk[:BLOCK].astype(BF16)
                halo_out[1, :, f] = gv[:BLOCK].astype(BF16)
                gk_acc[pl.ds(0, BLOCK), f] = gk[BLOCK:]
                gv_acc[pl.ds(0, BLOCK), f] = gv[BLOCK:]
            else:
                gs_sum[h] += gs
                gk_acc[pl.ds(0, BLOCK), f] += gk[:BLOCK]
                gv_acc[pl.ds(0, BLOCK), f] += gv[:BLOCK]
                gk_acc[pl.ds(BLOCK, BLOCK), f] = gk[BLOCK:]
                gv_acc[pl.ds(BLOCK, BLOCK), f] = gv[BLOCK:]
            return carry

        lax.fori_loop(0, HEADS, one, 0)

    back(0)
    g_halo = halo_copy(2, halo_out, halo_in, before)
    g_halo.start()
    back(1)

    mixed = ((stage_a, 2), (stage_b, 0)), ((stage_b, 1), (stage_b, 2))
    exchange(4, mixed, ((stage_b, gq_low),), send_in)

    def buckets_of(h, carry):
        gs = gs_sum[h]
        for k in range(BUCKETS):
            picked = jnp.where(bucket == k, gs, 0.0)
            part[pl.ds(h * BUCKETS + k, 1), :] = jnp.sum(picked, axis=0, keepdims=True)
        return carry

    lax.fori_loop(0, HEADS, buckets_of, 0)
    sums = jnp.sum(part[...], axis=1, keepdims=True)
    lines = [eye_turn(sums[r * 128 : (r + 1) * 128]) for r in range(2)]
    first_total = jnp.concatenate(lines + [jnp.zeros((6, 128), F32)], axis=0)

    rounds = (
        (NY * NC, y * NC + c, lambda i: (grp, place(x, z, i // NC, i % NC))),
        (NZ, z, lambda i: (grp, place(x, i, y, c))),
        (NX, x, lambda i: (grp, place(i, z, y, c))),
        (BATCH, grp, lambda i: (i, me)),
    )

    def round_start(r, value):
        n, mine, device = rounds[r]
        cur[r] = value
        red[r, mine] = value
        for d in range(1, n):
            pltpu.make_async_remote_copy(
                src_ref=cur.at[r],
                dst_ref=red.at[r, mine],
                send_sem=red_send.at[r],
                recv_sem=red_recv.at[r],
                device_id=device((mine + d) % n),
                device_id_type=MESH,
            ).start()

    def round_end(r):
        n = rounds[r][0]
        wait_bytes(red.at[r, pl.ds(0, n - 1)], red_recv.at[r])
        total = red[r, 0]
        for i in range(1, n):
            total = total + red[r, i]
        return total

    round_start(0, first_total)

    g_halo.wait_recv()
    for acc, low, i in ((gk_acc, gk_low, 0), (gv_acc, gv_low, 1)):
        low[:BLOCK, :] = acc[:BLOCK, :].astype(BF16)
        low[BLOCK:, :] = (acc[BLOCK:, :] + halo_in[i].astype(F32)).astype(BF16)
    exchange(5, by_two(stage_a, stage_b), ((stage_a, gk_low), (stage_b, gv_low)), send_in)

    round_start(1, round_end(0))
    round_start(2, round_end(1))
    def put_gate(f, v):
        gg_out[:, f] = (c_in[:, f].astype(F32) * v).astype(BF16)

    def put_gq(f, v):
        gq_out[:, f] = v.astype(BF16)

    def put_gk(f, v):
        gk_out[:, f] = v.astype(BF16)

    def put_gv(f, v):
        gv_out[:, f] = v.astype(BF16)

    arrived(3)
    unpack(recv[3], (((stage_a, 0), (stage_a, 1)),))
    arrived(4)
    unpack(recv[4], mixed)
    unstage(stage_a, land, put_gate)
    unstage(stage_b, land, put_gq)
    round_start(3, round_end(2))
    total = round_end(3) * (1.0 / math.sqrt(BATCH * PEERS * ROWS))
    for h in range(HEADS):
        at = h % 4 * BUCKETS
        bias_out[h : h + 1, :] = total[h // 4 : h // 4 + 1, at : at + BUCKETS]

    arrived(5)
    unpack(recv[5], by_two(stage_a, stage_b))
    unstage(stage_a, land, put_gk)
    unstage(stage_b, land, put_gv)

    for group in range(6):
        n = send[group].shape[0] // PEERS
        wait_bytes(send[group].at[pl.ds(n, (PEERS - 1) * n)], send_sem.at[group])
    k_halo.wait_send()
    v_halo.wait_send()
    g_halo.wait_send()
    for r in range(4):
        wait_bytes(red.at[r, pl.ds(0, rounds[r][0] - 1)], red_send.at[r])


def body(queries, keys, values, gates, cotangent, rel_bias, lengths, send_counts, block_pattern):
    vmem = pl.BlockSpec(memory_space=pltpu.VMEM)
    smem = pl.BlockSpec(memory_space=pltpu.SMEM)
    event = jax.ShapeDtypeStruct((ROWS, WIDTH), BF16)
    wide = pltpu.VMEM((ROWS, WIDTH), F32)
    low = pltpu.VMEM((ROWS, WIDTH), BF16)
    stage = pltpu.VMEM((LINES * CHUNKS, 128), F32)
    buffers = [pltpu.VMEM((PEERS * n, 16, 128), BF16) for n in (3, 2, 1, 1, 2, 3)]
    gq, gk, gv, gg, bias = pl.pallas_call(
        kernel,
        out_shape=(event, event, event, event, jax.ShapeDtypeStruct((HEADS, BUCKETS), F32)),
        in_specs=[vmem] * 5 + [smem] * 3 + [vmem],
        out_specs=(vmem,) * 5,
        scratch_shapes=buffers * 2
        + [stage, stage]
        + [pltpu.VMEM((LINES, ROWS), BF16)] * 2
        + [pltpu.VMEM((ROWS, LINES), BF16)] * 2
        + [low] * 5
        + [low, pltpu.VMEM((ROWS + BLOCK, WIDTH), BF16), pltpu.VMEM((ROWS + BLOCK, WIDTH), BF16), wide]
        + [
            pltpu.VMEM((ROWS, 128), F32),
            pltpu.VMEM((2, HEADS, BLOCK, SPAN), BF16),
            pltpu.VMEM((2, HEADS, BLOCK, SPAN), F32),
            pltpu.VMEM((HEADS, BLOCK, SPAN), F32),
            pltpu.VMEM((2, BLOCK, SPAN), F32),
        ]
        + [wide, low, wide, wide]
        + [
            pltpu.VMEM((2, BLOCK, WIDTH), BF16),
            pltpu.VMEM((2, BLOCK, WIDTH), BF16),
            pltpu.VMEM((HEADS, BLOCK, SPAN), F32),
            pltpu.VMEM((HEADS * BUCKETS, SPAN), F32),
            pltpu.VMEM((4, 8, 8, 128), F32),
            pltpu.VMEM((4, 8, 128), F32),
            pltpu.SemaphoreType.DMA((6,)),
            pltpu.SemaphoreType.DMA((6,)),
            pltpu.SemaphoreType.DMA((3,)),
            pltpu.SemaphoreType.DMA((3,)),
            pltpu.SemaphoreType.DMA((4,)),
            pltpu.SemaphoreType.DMA((4,)),
            pltpu.SemaphoreType.REGULAR,
        ],
        compiler_params=pltpu.CompilerParams(
            collective_id=0, has_side_effects=True, vmem_limit_bytes=56 * 1024 * 1024
        ),
    )(
        queries[0], keys[0], values[0], gates[0], cotangent[0],
        rel_bias, lengths, block_pattern, send_counts[0],
    )
    return gq[None], gk[None], gv[None], gg[None], bias


def solution(mesh):
    event = P("batch", "ctx", None)
    return jax.shard_map(
        body,
        mesh=mesh,
        in_specs=(event,) * 5 + (P(), P("batch", None), P("batch", None, None), event),
        out_specs=(event,) * 4 + (P(),),
        check_vma=False,
    )
```

```python
import math

import jax
import jax.numpy as jnp
from jax import lax
from jax.experimental import pallas as pl
from jax.experimental.pallas import tpu as pltpu
from jax.sharding import PartitionSpec as P

MESH = pl.DeviceIdType.MESH
F32 = jnp.float32
BF16 = jnp.bfloat16

NX, NZ, NY, NC = 4, 8, 2, 2
PEERS = NX * NZ * NY * NC
BATCH = 4
ROWS = 256
WIDTH = 1024
HEADS = 8
SIZE = 128
CHUNKS = WIDTH // 128
BLOCK = 128
SPAN = 256
BUCKETS = 32
SLOTS = 3
EPS = 1e-05
VMEM = 56 * 1024 * 1024
LINES = PEERS * SLOTS
STEP = 16
SCALE = SIZE ** (-0.5)


def coords(me):
    return me // (NZ * NY * NC), (me // (NY * NC)) % NZ, (me // NC) % NY, me % NC


def place(x, z, y, c):
    return ((x * NZ + z) * NY + y) * NC + c


def partner(me, k):
    x, z, y, c = coords(me)
    dx, dz, dy, dc = coords(k)
    return place((x + dx) % NX, (z + dz) % NZ, (y + dy) % NY, (c + dc) % NC)


def partners_of(me, k, sign):
    x, z, y, c = coords(me)
    dx, dz, dy, dc = k >> 5, (k >> 2) & 7, (k >> 1) & 1, k & 1
    return place((x + sign * dx) & 3, (z + sign * dz) & 7, (y + dy) & 1, (c + dc) & 1)


def eye_turn(vector):
    eye = lax.broadcasted_iota(jnp.int32, (128, 128), 0) == lax.broadcasted_iota(jnp.int32, (128, 128), 1)
    return jnp.sum(jnp.where(eye, vector, 0.0), axis=1 if vector.shape[0] == 1 else 0, keepdims=True)


def travel(me, row, col, axis, sign, only=None):
    def offset(line):
        return (line * 171) >> 9 if only is None else line

    lines = LINES if only is None else PEERS
    shape = (lines, 128) if axis == 0 else (128, lines)
    device = lax.broadcasted_iota(jnp.int32, shape, 1 - axis)
    along = lax.broadcasted_iota(jnp.int32, shape, axis)
    same = partners_of(me, offset(along), sign) == device
    pairs = (128, 128)
    below = lax.broadcasted_iota(jnp.int32, pairs, 1 - axis) < lax.broadcasted_iota(jnp.int32, pairs, axis)
    counts = row if axis == 0 else col
    lower = jnp.sum(jnp.where(below, counts, 0.0), axis=1 - axis, keepdims=True)
    lower = eye_turn(lower)
    count = jnp.sum(jnp.where(same, counts, 0.0), axis=1 - axis, keepdims=True)
    start = jnp.sum(jnp.where(same, lower, 0.0), axis=1 - axis, keepdims=True)
    line = lax.broadcasted_iota(jnp.int32, count.shape, axis)
    slot = (line - offset(line) * SLOTS).astype(F32) if only is None else float(only)
    index = jnp.where(slot < count, start + slot, -1.0)
    full = (lines, ROWS) if axis == 0 else (ROWS, lines)
    rows = lax.broadcasted_iota(jnp.int32, full, 1 - axis).astype(F32)
    return jnp.where(rows == index, 1.0, 0.0).astype(BF16)


def unstage(src, pick, write):
    for c in range(CHUNKS):
        rows = src[pl.ds(c, pick.shape[1], stride=CHUNKS), :].astype(BF16)
        write(slice(c * 128, (c + 1) * 128), matmul(pick[...], rows, 1, 0))


def unpack(recv, tiles, slots=SLOTS):
    step = 4

    def some(i, carry):
        for j in range(step):
            k = i * step + j
            for t, halves in enumerate(tiles):
                tile = recv[k * len(tiles) + t].astype(F32)
                for h, (buffer, slot) in enumerate(halves):
                    off = pl.multiple_of((k * slots + slot) * CHUNKS, CHUNKS)
                    buffer[pl.ds(off, CHUNKS), :] = tile[h * CHUNKS : (h + 1) * CHUNKS]
        return carry

    lax.fori_loop(0, PEERS // step, some, 0)


def wait_bytes(ref, sem):
    pltpu.make_async_copy(ref, ref, sem).wait()


def matmul(a, b, ca, cb):
    return lax.dot_general(a, b, (((ca,), (cb,)), ((), ())), preferred_element_type=F32)


def kernel(
    q_hbm, k_hbm, v_hbm, g_hbm, c_hbm, rel, lengths, pattern, counts,
    gq_hbm, gk_hbm, gv_hbm, gg_hbm, bias_out,
    send_0, send_1, send_2, send_3, send_4, send_5, send_6,
    recv_0, recv_1, recv_2, recv_3, recv_4, recv_5, recv_6,
    q_in, k_in, v_in, g_in, c_in, gq_out, gk_out, gv_out, gg_out,
    stage_a, stage_b, send_out, send_in, settle, land, land_last, gn_low, n_low, gq_low, gk_low, gv_low,
    q_own, k_ext, v_ext, gn_own, inv, a_all, d_all, table, mask,
    o_all, go_all, gk_acc, gv_acc, halo_out, halo_in, gs_sum, part, red, cur,
    send_sem, recv_sem, halo_send, halo_recv, red_send, red_recv, ready, in_sem, out_sem,
):
    send = (send_0, send_1, send_2, send_3, send_4, send_5, send_6)
    recv = (recv_0, recv_1, recv_2, recv_3, recv_4, recv_5, recv_6)
    me = lax.axis_index("ctx")
    grp = lax.axis_index("batch")
    x, z, y, c = coords(me)

    def ctx(i):
        return {"device_id": (grp, i), "device_id_type": MESH}

    barrier = pltpu.get_barrier_semaphore()
    line = [place(x, (z + d) % NZ, y, c) for d in range(1, NZ)]
    plane = [
        place((x + dx) % NX, z, (y + dy) % NY, (c + dc) % NC)
        for dx in range(NX) for dy in range(NY) for dc in range(NC)
    ][1:]
    for to in line + plane:
        pl.semaphore_signal(barrier, inc=1, **ctx(to))
    for d in range(1, BATCH):
        pl.semaphore_signal(barrier, inc=1, device_id=((grp + d) % BATCH, me), device_id_type=MESH)

    loads = [
        pltpu.make_async_copy(src, dst, in_sem.at[i])
        for i, (src, dst) in enumerate(
            ((k_hbm, k_in), (v_hbm, v_in), (c_hbm, c_in), (g_hbm, g_in), (q_hbm, q_in))
        )
    ]
    for load in loads:
        load.start()

    def leave(i, src, dst):
        copy = pltpu.make_async_copy(src, dst, out_sem.at[i])
        copy.start()
        return copy

    def exchange(group, tiles, staged, pick, gate=None):
        out, into, n = send[group], recv[group], len(tiles)

        def pack(dst, k):
            for t, halves in enumerate(tiles):
                pieces = []
                for buffer, slot in halves:
                    off = pl.multiple_of((k * SLOTS + slot) * CHUNKS, CHUNKS)
                    pieces.append(buffer[pl.ds(off, CHUNKS), :])
                dst[k * n + t] = jnp.concatenate(pieces, axis=0).astype(BF16)

        def one(k, carry):
            pack(out, k)
            pltpu.make_async_remote_copy(
                src_ref=out.at[pl.ds(k * n, n)],
                dst_ref=into.at[pl.ds(k * n, n)],
                send_sem=send_sem.at[group],
                recv_sem=recv_sem.at[group],
                **ctx(partner(me, k)),
            ).start()
            return carry

        def stage(i):
            for buffer, value in staged:
                lines = pl.ds(pl.multiple_of(i * STEP * SLOTS, STEP * SLOTS), STEP * SLOTS)
                rows = matmul(pick[lines, :], value[...], 1, 0)
                for f in range(CHUNKS):
                    to = pl.ds(i * STEP * SLOTS * CHUNKS + f, STEP * SLOTS, stride=CHUNKS)
                    buffer[to, :] = rows[:, f * 128 : (f + 1) * 128]

        def chunk(i, carry):
            stage(i)
            return lax.fori_loop(i * STEP, i * STEP + STEP, one, carry)

        stage(0)
        if gate is not None:
            gate()
        lax.fori_loop(1, STEP, one, 0)
        pack(into, 0)
        lax.fori_loop(1, PEERS // STEP, chunk, 0)

    def arrived(group):
        n = recv[group].shape[0] // PEERS
        wait_bytes(recv[group].at[pl.ds(n, (PEERS - 1) * n)], recv_sem.at[group])

    def halo_copy(i, src, dst, to):
        return pltpu.make_async_remote_copy(
            src_ref=src, dst_ref=dst, send_sem=halo_send.at[i], recv_sem=halo_recv.at[i], **ctx(to)
        )

    pl.semaphore_wait(barrier, len(line) + len(plane) + BATCH - 1)
    for to in line:
        pl.semaphore_signal(ready, inc=1, **ctx(to))

    out_row = counts[pl.ds(me, 1), :].astype(F32)
    lane = lax.broadcasted_iota(jnp.int32, (PEERS, PEERS), 1)
    in_col = jnp.sum(jnp.where(lane == me, counts[...].astype(F32), 0.0), axis=1, keepdims=True)
    out_col, in_row = eye_turn(out_row), eye_turn(in_col)
    send_out[...] = travel(me, out_row, out_col, 0, 1)

    by_two = lambda a, b: (((a, 0), (b, 0)), ((a, 1), (b, 1)), ((a, 2), (b, 2)))
    loads[0].wait()
    loads[1].wait()
    everyone = lambda: pl.semaphore_wait(ready, len(line))
    exchange(0, by_two(stage_a, stage_b), ((stage_a, k_in), (stage_b, v_in)), send_out, everyone)
    for load in loads[2:]:
        load.wait()
    gn_low[...] = (c_in[...].astype(F32) * g_in[...].astype(F32)).astype(BF16)
    rest = ((stage_b, 1), (stage_b, 2)),
    full = ((stage_a, 0), (stage_a, 1)), ((stage_a, 2), (stage_b, 0))
    exchange(1, full, ((stage_a, q_in), (stage_b, gn_low)), send_out)
    exchange(2, rest, (), send_out)
    settle[...] = travel(me, in_row, in_col, 1, -1)

    row_i = lax.broadcasted_iota(jnp.int32, (BLOCK, SPAN), 0)
    col_c = lax.broadcasted_iota(jnp.int32, (BLOCK, SPAN), 1)
    bucket = (row_i + BLOCK - col_c) >> 3

    def bias_of(h, carry):
        full = jnp.zeros((BLOCK, SPAN), F32)
        for k in range(BUCKETS):
            full = jnp.where(bucket == k, rel[h, k], full)
        table[h] = full
        return carry

    lax.fori_loop(0, HEADS, bias_of, 0)
    for b in range(2):
        pos_q = me * ROWS + b * BLOCK + row_i
        pos_k = me * ROWS + (b - 1) * BLOCK + col_c
        hist_q = jnp.zeros((BLOCK, SPAN), jnp.int32)
        hist_k = jnp.zeros((BLOCK, SPAN), jnp.int32)
        end = jnp.int32(0)
        for i in range(lengths.shape[1]):
            end = end + lengths[0, i]
            hist_q = hist_q + (pos_q >= end).astype(jnp.int32)
            hist_k = hist_k + (pos_k >= end).astype(jnp.int32)
        flag = jnp.where(col_c >= BLOCK, pattern[0, b, 0], pattern[0, b, 1])
        live = (pos_k <= pos_q) & (pos_k >= 0) & (hist_q == hist_k) & (flag > 0)
        mask[b] = jnp.where(live, 1.0 / SPAN, 0.0).astype(F32)

    def put_q(f, v):
        q_own[:, f] = v.astype(BF16)

    def put_k(f, v):
        k_ext[BLOCK:, f] = v.astype(BF16)

    def put_v(f, v):
        v_ext[BLOCK:, f] = v.astype(BF16)

    def put_gn(f, v):
        gn_own[:, f] = v

    after, before = (me + 1) % PEERS, (me + PEERS - 1) % PEERS
    arrived(0)
    unpack(recv[0], by_two(stage_a, stage_b))
    unstage(stage_a, settle, put_k)
    k_halo = halo_copy(0, k_ext.at[pl.ds(ROWS, BLOCK)], k_ext.at[pl.ds(0, BLOCK)], after)
    k_halo.start()
    unstage(stage_b, settle, put_v)
    v_halo = halo_copy(1, v_ext.at[pl.ds(ROWS, BLOCK)], v_ext.at[pl.ds(0, BLOCK)], after)
    v_halo.start()
    send_in[...] = travel(me, in_row, in_col, 0, 1)
    land[...] = travel(me, out_row, out_col, 1, -1)
    land_last[...] = travel(me, out_row, out_col, 1, -1, SLOTS - 1)

    def forward(b):
        def one(h, carry):
            f = pl.ds(pl.multiple_of(h * SIZE, SIZE), SIZE)
            raw = matmul(q_own[pl.ds(b * BLOCK, BLOCK), f], k_ext[pl.ds(b * BLOCK, SPAN), f], 1, 1)
            s = raw * SCALE + table[h]
            sig = jax.nn.sigmoid(s)
            m = mask[b]
            a = (s * sig * m).astype(BF16)
            a_all[b, h] = a
            d_all[b, h] = sig * (1.0 + s * (1.0 - sig)) * m
            o_all[pl.ds(b * BLOCK, BLOCK), f] = matmul(a, v_ext[pl.ds(b * BLOCK, SPAN), f], 1, 0)
            return carry

        lax.fori_loop(0, HEADS, one, 0, unroll=2)

    arrived(1)
    unpack(recv[1], full)
    unstage(stage_a, settle, put_q)
    forward(1)
    k_halo.wait_recv()
    v_halo.wait_recv()
    forward(0)

    def norm(i, carry):
        rows = pl.ds(pl.multiple_of(i * 32, 32), 32)
        out = o_all[rows, :]
        center = out - jnp.mean(out, axis=-1, keepdims=True)
        inverse = lax.rsqrt(jnp.mean(center * center, axis=-1, keepdims=True) + EPS)
        normed = center * inverse
        o_all[rows, :] = normed
        n_low[rows, :] = normed.astype(BF16)
        inv[rows, :] = jnp.broadcast_to(inverse, (32, 128))
        return carry

    lax.fori_loop(0, ROWS // 32, norm, 0)
    exchange(3, (((stage_a, 0), (stage_a, 1)),), ((stage_a, n_low),), send_in)

    arrived(2)
    unpack(recv[2], rest)
    unstage(stage_b, settle, put_gn)

    def norm_back(i, carry):
        rows = pl.ds(pl.multiple_of(i * 32, 32), 32)
        normed = o_all[rows, :]
        gn = gn_own[rows, :]
        go = (
            gn
            - jnp.mean(gn, axis=-1, keepdims=True)
            - normed * jnp.mean(gn * normed, axis=-1, keepdims=True)
        ) * inv[rows, :1]
        go_all[rows, :] = go.astype(BF16)
        return carry

    lax.fori_loop(0, ROWS // 32, norm_back, 0)

    def back(b):
        def one(h, carry):
            f = pl.ds(pl.multiple_of(h * SIZE, SIZE), SIZE)
            own = pl.ds(b * BLOCK, BLOCK)
            win = pl.ds(b * BLOCK, SPAN)
            go = go_all[own, f]
            gs = matmul(go, v_ext[win, f], 1, 1) * d_all[b, h]
            low = gs.astype(BF16)
            gq_low[own, f] = (matmul(low, k_ext[win, f], 1, 0) * SCALE).astype(BF16)
            gk = matmul(low, q_own[own, f], 0, 0) * SCALE
            gv = matmul(a_all[b, h], go, 0, 0)
            if b == 0:
                gs_sum[h] = gs
                halo_out[0, :, f] = gk[:BLOCK].astype(BF16)
                halo_out[1, :, f] = gv[:BLOCK].astype(BF16)
                gk_acc[pl.ds(0, BLOCK), f] = gk[BLOCK:]
                gv_acc[pl.ds(0, BLOCK), f] = gv[BLOCK:]
            else:
                gs_sum[h] += gs
                gk_acc[pl.ds(0, BLOCK), f] += gk[:BLOCK]
                gv_acc[pl.ds(0, BLOCK), f] += gv[:BLOCK]
                gk_acc[pl.ds(BLOCK, BLOCK), f] = gk[BLOCK:]
                gv_acc[pl.ds(BLOCK, BLOCK), f] = gv[BLOCK:]
            return carry

        lax.fori_loop(0, HEADS, one, 0, unroll=2)

    back(0)
    g_halo = halo_copy(2, halo_out, halo_in, before)
    g_halo.start()
    back(1)

    mixed = ((stage_a, 2), (stage_b, 0)), ((stage_b, 1), (stage_b, 2))
    exchange(4, mixed, ((stage_b, gq_low),), send_in)

    def buckets_of(h, carry):
        gs = gs_sum[h]
        for k in range(BUCKETS):
            picked = jnp.where(bucket == k, gs, 0.0)
            part[pl.ds(h * BUCKETS + k, 1), :] = jnp.sum(picked, axis=0, keepdims=True)
        return carry

    lax.fori_loop(0, HEADS, buckets_of, 0)
    sums = jnp.sum(part[...], axis=1, keepdims=True)
    lines = [eye_turn(sums[r * 128 : (r + 1) * 128]) for r in range(2)]
    first_total = jnp.concatenate(lines + [jnp.zeros((6, 128), F32)], axis=0)

    rounds = (
        (NY * NC, y * NC + c, lambda i: (grp, place(x, z, i // NC, i % NC))),
        (NZ, z, lambda i: (grp, place(x, i, y, c))),
        (NX, x, lambda i: (grp, place(i, z, y, c))),
        (BATCH, grp, lambda i: (i, me)),
    )

    def round_start(r, value):
        n, mine, device = rounds[r]
        cur[r] = value
        red[r, mine] = value
        for d in range(1, n):
            pltpu.make_async_remote_copy(
                src_ref=cur.at[r],
                dst_ref=red.at[r, mine],
                send_sem=red_send.at[r],
                recv_sem=red_recv.at[r],
                device_id=device((mine + d) % n),
                device_id_type=MESH,
            ).start()

    def round_end(r):
        n = rounds[r][0]
        wait_bytes(red.at[r, pl.ds(0, n - 1)], red_recv.at[r])
        total = red[r, 0]
        for i in range(1, n):
            total = total + red[r, i]
        return total

    round_start(0, first_total)

    g_halo.wait_recv()
    for acc, low, i in ((gk_acc, gk_low, 0), (gv_acc, gv_low, 1)):
        low[:BLOCK, :] = acc[:BLOCK, :].astype(BF16)
        low[BLOCK:, :] = (acc[BLOCK:, :] + halo_in[i].astype(F32)).astype(BF16)
    first_two = by_two(stage_a, stage_b)[:2]
    exchange(5, first_two, ((stage_a, gk_low), (stage_b, gv_low)), send_in)
    exchange(6, by_two(stage_a, stage_b)[2:], (), send_in)

    round_start(1, round_end(0))
    round_start(2, round_end(1))
    def put_gate(f, v):
        gg_out[:, f] = (c_in[:, f].astype(F32) * v).astype(BF16)

    def put_gq(f, v):
        gq_out[:, f] = v.astype(BF16)

    def put_gk(f, v):
        gk_acc[:, f] = v

    def put_gv(f, v):
        gv_acc[:, f] = v

    def end_gk(f, v):
        gk_out[:, f] = (gk_acc[:, f] + v).astype(BF16)

    def end_gv(f, v):
        gv_out[:, f] = (gv_acc[:, f] + v).astype(BF16)

    arrived(3)
    unpack(recv[3], (((stage_a, 0), (stage_a, 1)),))
    arrived(4)
    unpack(recv[4], mixed)
    unstage(stage_a, land, put_gate)
    gone = [leave(0, gg_out, gg_hbm)]
    unstage(stage_b, land, put_gq)
    gone.append(leave(1, gq_out, gq_hbm))
    lines = lax.broadcasted_iota(jnp.int32, (ROWS, LINES), 1)
    early = lines - ((lines * 171) >> 9) * SLOTS < SLOTS - 1
    land[...] = jnp.where(early, land[...].astype(F32), 0.0).astype(BF16)
    round_start(3, round_end(2))
    total = round_end(3) * (1.0 / math.sqrt(BATCH * PEERS * ROWS))
    for h in range(HEADS):
        at = h % 4 * BUCKETS
        bias_out[h : h + 1, :] = total[h // 4 : h // 4 + 1, at : at + BUCKETS]

    arrived(5)
    unpack(recv[5], first_two)
    unstage(stage_a, land, put_gk)
    unstage(stage_b, land, put_gv)
    arrived(6)
    unpack(recv[6], (((stage_a, 0), (stage_b, 0)),), 1)
    unstage(stage_a, land_last, end_gk)
    gone.append(leave(2, gk_out, gk_hbm))
    unstage(stage_b, land_last, end_gv)
    gone.append(leave(3, gv_out, gv_hbm))

    for copy in gone:
        copy.wait()
    for group in range(7):
        n = send[group].shape[0] // PEERS
        wait_bytes(send[group].at[pl.ds(n, (PEERS - 1) * n)], send_sem.at[group])
    k_halo.wait_send()
    v_halo.wait_send()
    g_halo.wait_send()
    for r in range(4):
        wait_bytes(red.at[r, pl.ds(0, rounds[r][0] - 1)], red_send.at[r])


def hand_over(*refs):
    for i in range(5):
        refs[5 + i][...] = refs[i][...]


def body(queries, keys, values, gates, cotangent, rel_bias, lengths, send_counts, block_pattern):
    vmem = pl.BlockSpec(memory_space=pltpu.VMEM)
    smem = pl.BlockSpec(memory_space=pltpu.SMEM)
    hbm = pl.BlockSpec(memory_space=pl.ANY)
    event = jax.ShapeDtypeStruct((ROWS, WIDTH), BF16)
    wide = pltpu.VMEM((ROWS, WIDTH), F32)
    low = pltpu.VMEM((ROWS, WIDTH), BF16)
    stage = pltpu.VMEM((LINES * CHUNKS, 128), F32)
    buffers = [pltpu.VMEM((PEERS * n, 16, 128), BF16) for n in (3, 2, 1, 1, 2, 2, 1)]
    results = pl.pallas_call(
        kernel,
        out_shape=(event, event, event, event, jax.ShapeDtypeStruct((HEADS, BUCKETS), F32)),
        in_specs=[hbm] * 5 + [smem] * 3 + [vmem],
        out_specs=(hbm,) * 4 + (vmem,),
        scratch_shapes=buffers * 2
        + [low] * 9
        + [stage, stage]
        + [pltpu.VMEM((LINES, ROWS), BF16)] * 2
        + [pltpu.VMEM((ROWS, LINES), BF16)] * 2
        + [pltpu.VMEM((ROWS, PEERS), BF16)]
        + [low] * 5
        + [low, pltpu.VMEM((ROWS + BLOCK, WIDTH), BF16), pltpu.VMEM((ROWS + BLOCK, WIDTH), BF16), wide]
        + [
            pltpu.VMEM((ROWS, 128), F32),
            pltpu.VMEM((2, HEADS, BLOCK, SPAN), BF16),
            pltpu.VMEM((2, HEADS, BLOCK, SPAN), F32),
            pltpu.VMEM((HEADS, BLOCK, SPAN), F32),
            pltpu.VMEM((2, BLOCK, SPAN), F32),
        ]
        + [wide, low, wide, wide]
        + [
            pltpu.VMEM((2, BLOCK, WIDTH), BF16),
            pltpu.VMEM((2, BLOCK, WIDTH), BF16),
            pltpu.VMEM((HEADS, BLOCK, SPAN), F32),
            pltpu.VMEM((HEADS * BUCKETS, SPAN), F32),
            pltpu.VMEM((4, 8, 8, 128), F32),
            pltpu.VMEM((4, 8, 128), F32),
            pltpu.SemaphoreType.DMA((7,)),
            pltpu.SemaphoreType.DMA((7,)),
            pltpu.SemaphoreType.DMA((3,)),
            pltpu.SemaphoreType.DMA((3,)),
            pltpu.SemaphoreType.DMA((4,)),
            pltpu.SemaphoreType.DMA((4,)),
            pltpu.SemaphoreType.REGULAR,
            pltpu.SemaphoreType.DMA((5,)),
            pltpu.SemaphoreType.DMA((4,)),
        ],
        compiler_params=pltpu.CompilerParams(
            collective_id=0, has_side_effects=True, vmem_limit_bytes=VMEM
        ),
    )(
        queries[0], keys[0], values[0], gates[0], cotangent[0],
        rel_bias, lengths, block_pattern, send_counts[0],
    )
    strips = [pl.BlockSpec((ROWS // 4, WIDTH), lambda i: (i, 0))] * 4
    strips.append(pl.BlockSpec((HEADS, BUCKETS), lambda i: (0, 0)))
    gq, gk, gv, gg, bias = pl.pallas_call(
        hand_over,
        out_shape=[jax.ShapeDtypeStruct(r.shape, r.dtype) for r in results],
        grid=(4,),
        in_specs=strips,
        out_specs=strips,
        compiler_params=pltpu.CompilerParams(vmem_limit_bytes=VMEM),
    )(*results)
    return gq[None], gk[None], gv[None], gg[None], bias


def solution(mesh):
    event = P("batch", "ctx", None)
    return jax.shard_map(
        body,
        mesh=mesh,
        in_specs=(event,) * 5 + (P(), P("batch", None), P("batch", None, None), event),
        out_specs=(event,) * 4 + (P(),),
        check_vma=False,
    )
```

```python
import math

import jax
import jax.numpy as jnp
from jax import lax
from jax.experimental import pallas as pl
from jax.experimental.pallas import tpu as pltpu
from jax.sharding import PartitionSpec as P

MESH = pl.DeviceIdType.MESH
F32 = jnp.float32
BF16 = jnp.bfloat16

NX, NZ, NY, NC = 4, 8, 2, 2
PEERS = NX * NZ * NY * NC
BATCH = 4
ROWS = 256
WIDTH = 1024
HEADS = 8
SIZE = 128
CHUNKS = WIDTH // 128
BLOCK = 128
SPAN = 256
BUCKETS = 32
SLOTS = 3
EPS = 1e-05
VMEM = 56 * 1024 * 1024
LINES = PEERS * SLOTS
STEP = 16
SCALE = SIZE ** (-0.5)


def coords(me):
    return me // (NZ * NY * NC), (me // (NY * NC)) % NZ, (me // NC) % NY, me % NC


def place(x, z, y, c):
    return ((x * NZ + z) * NY + y) * NC + c


def partner(me, k):
    x, z, y, c = coords(me)
    dx, dz, dy, dc = coords(k)
    return place((x + dx) % NX, (z + dz) % NZ, (y + dy) % NY, (c + dc) % NC)


def partners_of(me, k, sign):
    x, z, y, c = coords(me)
    dx, dz, dy, dc = k >> 5, (k >> 2) & 7, (k >> 1) & 1, k & 1
    return place((x + sign * dx) & 3, (z + sign * dz) & 7, (y + dy) & 1, (c + dc) & 1)


def eye_turn(vector):
    eye = lax.broadcasted_iota(jnp.int32, (128, 128), 0) == lax.broadcasted_iota(jnp.int32, (128, 128), 1)
    return jnp.sum(jnp.where(eye, vector, 0.0), axis=1 if vector.shape[0] == 1 else 0, keepdims=True)


def travel(me, row, col, axis, sign, only=None):
    def offset(line):
        return (line * 171) >> 9 if only is None else line

    lines = LINES if only is None else PEERS
    shape = (lines, 128) if axis == 0 else (128, lines)
    device = lax.broadcasted_iota(jnp.int32, shape, 1 - axis)
    along = lax.broadcasted_iota(jnp.int32, shape, axis)
    same = partners_of(me, offset(along), sign) == device
    pairs = (128, 128)
    below = lax.broadcasted_iota(jnp.int32, pairs, 1 - axis) < lax.broadcasted_iota(jnp.int32, pairs, axis)
    counts = row if axis == 0 else col
    lower = jnp.sum(jnp.where(below, counts, 0.0), axis=1 - axis, keepdims=True)
    lower = eye_turn(lower)
    count = jnp.sum(jnp.where(same, counts, 0.0), axis=1 - axis, keepdims=True)
    start = jnp.sum(jnp.where(same, lower, 0.0), axis=1 - axis, keepdims=True)
    line = lax.broadcasted_iota(jnp.int32, count.shape, axis)
    slot = (line - offset(line) * SLOTS).astype(F32) if only is None else float(only)
    index = jnp.where(slot < count, start + slot, -1.0)
    full = (lines, ROWS) if axis == 0 else (ROWS, lines)
    rows = lax.broadcasted_iota(jnp.int32, full, 1 - axis).astype(F32)
    return jnp.where(rows == index, 1.0, 0.0).astype(BF16)


def unstage(src, pick, write):
    for c in range(CHUNKS):
        rows = src[pl.ds(c, pick.shape[1], stride=CHUNKS), :].astype(BF16)
        write(slice(c * 128, (c + 1) * 128), matmul(pick[...], rows, 1, 0))


def unpack(recv, tiles, slots=SLOTS):
    step = 4

    def some(i, carry):
        for j in range(step):
            k = i * step + j
            for t, halves in enumerate(tiles):
                tile = recv[k * len(tiles) + t].astype(F32)
                for h, (buffer, slot) in enumerate(halves):
                    off = pl.multiple_of((k * slots + slot) * CHUNKS, CHUNKS)
                    buffer[pl.ds(off, CHUNKS), :] = tile[h * CHUNKS : (h + 1) * CHUNKS]
        return carry

    lax.fori_loop(0, PEERS // step, some, 0)


def wait_bytes(ref, sem):
    pltpu.make_async_copy(ref, ref, sem).wait()


def matmul(a, b, ca, cb):
    return lax.dot_general(a, b, (((ca,), (cb,)), ((), ())), preferred_element_type=F32)


def kernel(
    q_hbm, k_hbm, v_hbm, g_hbm, c_hbm, rel, lengths, pattern, counts,
    gq_hbm, gk_hbm, gv_hbm, gg_hbm, bias_out,
    send_0, send_1, send_2, send_3, send_4, send_5, send_6,
    recv_0, recv_1, recv_2, recv_3, recv_4, recv_5, recv_6,
    q_in, k_in, v_in, g_in, c_in, gq_out, gk_out, gv_out, gg_out,
    stage_a, stage_b, send_out, send_in, settle, land, land_last, gn_low, n_low, gq_low, gk_low, gv_low,
    q_own, k_ext, v_ext, gn_own, inv, a_all, d_all, table, mask,
    o_all, go_all, gk_acc, gv_acc, halo_out, halo_in, gs_sum, part, red, cur,
    send_sem, recv_sem, halo_send, halo_recv, red_send, red_recv, ready, in_sem, out_sem,
):
    send = (send_0, send_1, send_2, send_3, send_4, send_5, send_6)
    recv = (recv_0, recv_1, recv_2, recv_3, recv_4, recv_5, recv_6)
    me = lax.axis_index("ctx")
    grp = lax.axis_index("batch")
    x, z, y, c = coords(me)

    def ctx(i):
        return {"device_id": (grp, i), "device_id_type": MESH}

    barrier = pltpu.get_barrier_semaphore()
    line = [place(x, (z + d) % NZ, y, c) for d in range(1, NZ)]
    plane = [
        place((x + dx) % NX, z, (y + dy) % NY, (c + dc) % NC)
        for dx in range(NX) for dy in range(NY) for dc in range(NC)
    ][1:]
    for to in line + plane:
        pl.semaphore_signal(barrier, inc=1, **ctx(to))
    for d in range(1, BATCH):
        pl.semaphore_signal(barrier, inc=1, device_id=((grp + d) % BATCH, me), device_id_type=MESH)

    loads = [
        pltpu.make_async_copy(src, dst, in_sem.at[i])
        for i, (src, dst) in enumerate(
            ((k_hbm, k_in), (v_hbm, v_in), (c_hbm, c_in), (g_hbm, g_in), (q_hbm, q_in))
        )
    ]
    for load in loads:
        load.start()

    def leave(i, src, dst):
        copy = pltpu.make_async_copy(src, dst, out_sem.at[i])
        copy.start()
        return copy

    def exchange(group, tiles, staged, pick, gate=None):
        out, into, n = send[group], recv[group], len(tiles)

        def pack(dst, k):
            for t, halves in enumerate(tiles):
                pieces = []
                for buffer, slot in halves:
                    off = pl.multiple_of((k * SLOTS + slot) * CHUNKS, CHUNKS)
                    pieces.append(buffer[pl.ds(off, CHUNKS), :])
                dst[k * n + t] = jnp.concatenate(pieces, axis=0).astype(BF16)

        def one(k, carry):
            pack(out, k)
            pltpu.make_async_remote_copy(
                src_ref=out.at[pl.ds(k * n, n)],
                dst_ref=into.at[pl.ds(k * n, n)],
                send_sem=send_sem.at[group],
                recv_sem=recv_sem.at[group],
                **ctx(partner(me, k)),
            ).start()
            return carry

        def stage(i):
            for buffer, value in staged:
                lines = pl.ds(pl.multiple_of(i * STEP * SLOTS, STEP * SLOTS), STEP * SLOTS)
                rows = matmul(pick[lines, :], value[...], 1, 0)
                for f in range(CHUNKS):
                    to = pl.ds(i * STEP * SLOTS * CHUNKS + f, STEP * SLOTS, stride=CHUNKS)
                    buffer[to, :] = rows[:, f * 128 : (f + 1) * 128]

        def chunk(i, carry):
            stage(i)
            return lax.fori_loop(i * STEP, i * STEP + STEP, one, carry)

        stage(0)
        if gate is not None:
            gate()
        lax.fori_loop(1, STEP, one, 0)
        pack(into, 0)
        lax.fori_loop(1, PEERS // STEP, chunk, 0)

    def arrived(group):
        n = recv[group].shape[0] // PEERS
        wait_bytes(recv[group].at[pl.ds(n, (PEERS - 1) * n)], recv_sem.at[group])

    def halo_copy(i, src, dst, to):
        return pltpu.make_async_remote_copy(
            src_ref=src, dst_ref=dst, send_sem=halo_send.at[i], recv_sem=halo_recv.at[i], **ctx(to)
        )

    pl.semaphore_wait(barrier, len(line) + len(plane) + BATCH - 1)
    for to in line:
        pl.semaphore_signal(ready, inc=1, **ctx(to))

    out_row = counts[pl.ds(me, 1), :].astype(F32)
    lane = lax.broadcasted_iota(jnp.int32, (PEERS, PEERS), 1)
    in_col = jnp.sum(jnp.where(lane == me, counts[...].astype(F32), 0.0), axis=1, keepdims=True)
    out_col, in_row = eye_turn(out_row), eye_turn(in_col)
    send_out[...] = travel(me, out_row, out_col, 0, 1)

    by_two = lambda a, b: (((a, 0), (b, 0)), ((a, 1), (b, 1)), ((a, 2), (b, 2)))
    loads[0].wait()
    loads[1].wait()
    everyone = lambda: pl.semaphore_wait(ready, len(line))
    exchange(0, by_two(stage_a, stage_b), ((stage_a, k_in), (stage_b, v_in)), send_out, everyone)
    for load in loads[2:]:
        load.wait()
    gn_low[...] = (c_in[...].astype(F32) * g_in[...].astype(F32)).astype(BF16)
    rest = ((stage_b, 1), (stage_b, 2)),
    full = ((stage_a, 0), (stage_a, 1)), ((stage_a, 2), (stage_b, 0))
    exchange(1, full, ((stage_a, q_in), (stage_b, gn_low)), send_out)
    exchange(2, rest, (), send_out)
    settle[...] = travel(me, in_row, in_col, 1, -1)

    row_i = lax.broadcasted_iota(jnp.int32, (BLOCK, SPAN), 0)
    col_c = lax.broadcasted_iota(jnp.int32, (BLOCK, SPAN), 1)
    bucket = (row_i + BLOCK - col_c) >> 3

    def bias_of(h, carry):
        full = jnp.zeros((BLOCK, SPAN), F32)
        for k in range(BUCKETS):
            full = jnp.where(bucket == k, rel[h, k], full)
        table[h] = full
        return carry

    lax.fori_loop(0, HEADS, bias_of, 0)
    for b in range(2):
        pos_q = me * ROWS + b * BLOCK + row_i
        pos_k = me * ROWS + (b - 1) * BLOCK + col_c
        hist_q = jnp.zeros((BLOCK, SPAN), jnp.int32)
        hist_k = jnp.zeros((BLOCK, SPAN), jnp.int32)
        end = jnp.int32(0)
        for i in range(lengths.shape[1]):
            end = end + lengths[0, i]
            hist_q = hist_q + (pos_q >= end).astype(jnp.int32)
            hist_k = hist_k + (pos_k >= end).astype(jnp.int32)
        flag = jnp.where(col_c >= BLOCK, pattern[0, b, 0], pattern[0, b, 1])
        live = (pos_k <= pos_q) & (pos_k >= 0) & (hist_q == hist_k) & (flag > 0)
        mask[b] = jnp.where(live, 1.0 / SPAN, 0.0).astype(F32)

    def put_q(f, v):
        q_own[:, f] = v.astype(BF16)

    def put_k(f, v):
        k_ext[BLOCK:, f] = v.astype(BF16)

    def put_v(f, v):
        v_ext[BLOCK:, f] = v.astype(BF16)

    def put_gn(f, v):
        gn_own[:, f] = v

    after, before = (me + 1) % PEERS, (me + PEERS - 1) % PEERS
    arrived(0)
    unpack(recv[0], by_two(stage_a, stage_b))
    unstage(stage_a, settle, put_k)
    k_halo = halo_copy(0, k_ext.at[pl.ds(ROWS, BLOCK)], k_ext.at[pl.ds(0, BLOCK)], after)
    k_halo.start()
    unstage(stage_b, settle, put_v)
    v_halo = halo_copy(1, v_ext.at[pl.ds(ROWS, BLOCK)], v_ext.at[pl.ds(0, BLOCK)], after)
    v_halo.start()
    send_in[...] = travel(me, in_row, in_col, 0, 1)
    land[...] = travel(me, out_row, out_col, 1, -1)
    land_last[...] = travel(me, out_row, out_col, 1, -1, SLOTS - 1)

    def forward(b):
        def one(h, carry):
            f = pl.ds(pl.multiple_of(h * SIZE, SIZE), SIZE)
            raw = matmul(q_own[pl.ds(b * BLOCK, BLOCK), f], k_ext[pl.ds(b * BLOCK, SPAN), f], 1, 1)
            s = raw * SCALE + table[h]
            sig = jax.nn.sigmoid(s)
            m = mask[b]
            a = (s * sig * m).astype(BF16)
            a_all[b, h] = a
            d_all[b, h] = sig * (1.0 + s * (1.0 - sig)) * m
            o_all[pl.ds(b * BLOCK, BLOCK), f] = matmul(a, v_ext[pl.ds(b * BLOCK, SPAN), f], 1, 0)
            return carry

        lax.fori_loop(0, HEADS, one, 0, unroll=4)

    arrived(1)
    unpack(recv[1], full)
    unstage(stage_a, settle, put_q)
    forward(1)
    k_halo.wait_recv()
    v_halo.wait_recv()
    forward(0)

    def norm(i, carry):
        rows = pl.ds(pl.multiple_of(i * 32, 32), 32)
        out = o_all[rows, :]
        center = out - jnp.mean(out, axis=-1, keepdims=True)
        inverse = lax.rsqrt(jnp.mean(center * center, axis=-1, keepdims=True) + EPS)
        normed = center * inverse
        o_all[rows, :] = normed
        n_low[rows, :] = normed.astype(BF16)
        inv[rows, :] = jnp.broadcast_to(inverse, (32, 128))
        return carry

    lax.fori_loop(0, ROWS // 32, norm, 0, unroll=2)
    exchange(3, (((stage_a, 0), (stage_a, 1)),), ((stage_a, n_low),), send_in)

    arrived(2)
    unpack(recv[2], rest)
    unstage(stage_b, settle, put_gn)

    def norm_back(i, carry):
        rows = pl.ds(pl.multiple_of(i * 32, 32), 32)
        normed = o_all[rows, :]
        gn = gn_own[rows, :]
        go = (
            gn
            - jnp.mean(gn, axis=-1, keepdims=True)
            - normed * jnp.mean(gn * normed, axis=-1, keepdims=True)
        ) * inv[rows, :1]
        go_all[rows, :] = go.astype(BF16)
        return carry

    lax.fori_loop(0, ROWS // 32, norm_back, 0, unroll=2)

    def back(b):
        def one(h, carry):
            f = pl.ds(pl.multiple_of(h * SIZE, SIZE), SIZE)
            own = pl.ds(b * BLOCK, BLOCK)
            win = pl.ds(b * BLOCK, SPAN)
            go = go_all[own, f]
            gs = matmul(go, v_ext[win, f], 1, 1) * d_all[b, h]
            low = gs.astype(BF16)
            gq_low[own, f] = (matmul(low, k_ext[win, f], 1, 0) * SCALE).astype(BF16)
            gk = matmul(low, q_own[own, f], 0, 0) * SCALE
            gv = matmul(a_all[b, h], go, 0, 0)
            if b == 0:
                gs_sum[h] = gs
                halo_out[0, :, f] = gk[:BLOCK].astype(BF16)
                halo_out[1, :, f] = gv[:BLOCK].astype(BF16)
                gk_acc[pl.ds(0, BLOCK), f] = gk[BLOCK:]
                gv_acc[pl.ds(0, BLOCK), f] = gv[BLOCK:]
            else:
                gs_sum[h] += gs
                gk_acc[pl.ds(0, BLOCK), f] += gk[:BLOCK]
                gv_acc[pl.ds(0, BLOCK), f] += gv[:BLOCK]
                gk_acc[pl.ds(BLOCK, BLOCK), f] = gk[BLOCK:]
                gv_acc[pl.ds(BLOCK, BLOCK), f] = gv[BLOCK:]
            return carry

        lax.fori_loop(0, HEADS, one, 0, unroll=4)

    back(0)
    g_halo = halo_copy(2, halo_out, halo_in, before)
    g_halo.start()
    back(1)

    mixed = ((stage_a, 2), (stage_b, 0)), ((stage_b, 1), (stage_b, 2))
    exchange(4, mixed, ((stage_b, gq_low),), send_in)

    def buckets_of(h, carry):
        gs = gs_sum[h]
        for k in range(BUCKETS):
            picked = jnp.where(bucket == k, gs, 0.0)
            part[pl.ds(h * BUCKETS + k, 1), :] = jnp.sum(picked, axis=0, keepdims=True)
        return carry

    lax.fori_loop(0, HEADS, buckets_of, 0)
    sums = jnp.sum(part[...], axis=1, keepdims=True)
    lines = [eye_turn(sums[r * 128 : (r + 1) * 128]) for r in range(2)]
    first_total = jnp.concatenate(lines + [jnp.zeros((6, 128), F32)], axis=0)

    rounds = (
        (NY * NC, y * NC + c, lambda i: (grp, place(x, z, i // NC, i % NC))),
        (NZ, z, lambda i: (grp, place(x, i, y, c))),
        (NX, x, lambda i: (grp, place(i, z, y, c))),
        (BATCH, grp, lambda i: (i, me)),
    )

    def round_start(r, value):
        n, mine, device = rounds[r]
        cur[r] = value
        red[r, mine] = value
        for d in range(1, n):
            pltpu.make_async_remote_copy(
                src_ref=cur.at[r],
                dst_ref=red.at[r, mine],
                send_sem=red_send.at[r],
                recv_sem=red_recv.at[r],
                device_id=device((mine + d) % n),
                device_id_type=MESH,
            ).start()

    def round_end(r):
        n = rounds[r][0]
        wait_bytes(red.at[r, pl.ds(0, n - 1)], red_recv.at[r])
        total = red[r, 0]
        for i in range(1, n):
            total = total + red[r, i]
        return total

    round_start(0, first_total)

    g_halo.wait_recv()
    for acc, low, i in ((gk_acc, gk_low, 0), (gv_acc, gv_low, 1)):
        low[:BLOCK, :] = acc[:BLOCK, :].astype(BF16)
        low[BLOCK:, :] = (acc[BLOCK:, :] + halo_in[i].astype(F32)).astype(BF16)
    first_two = by_two(stage_a, stage_b)[:2]
    exchange(5, first_two, ((stage_a, gk_low), (stage_b, gv_low)), send_in)
    exchange(6, by_two(stage_a, stage_b)[2:], (), send_in)

    round_start(1, round_end(0))
    round_start(2, round_end(1))
    def put_gate(f, v):
        gg_out[:, f] = (c_in[:, f].astype(F32) * v).astype(BF16)

    def put_gq(f, v):
        gq_out[:, f] = v.astype(BF16)

    def put_gk(f, v):
        gk_acc[:, f] = v

    def put_gv(f, v):
        gv_acc[:, f] = v

    def end_gk(f, v):
        gk_out[:, f] = (gk_acc[:, f] + v).astype(BF16)

    def end_gv(f, v):
        gv_out[:, f] = (gv_acc[:, f] + v).astype(BF16)

    arrived(3)
    unpack(recv[3], (((stage_a, 0), (stage_a, 1)),))
    arrived(4)
    unpack(recv[4], mixed)
    unstage(stage_a, land, put_gate)
    gone = [leave(0, gg_out, gg_hbm)]
    unstage(stage_b, land, put_gq)
    gone.append(leave(1, gq_out, gq_hbm))
    lines = lax.broadcasted_iota(jnp.int32, (ROWS, LINES), 1)
    early = lines - ((lines * 171) >> 9) * SLOTS < SLOTS - 1
    land[...] = jnp.where(early, land[...].astype(F32), 0.0).astype(BF16)
    round_start(3, round_end(2))
    total = round_end(3) * (1.0 / math.sqrt(BATCH * PEERS * ROWS))
    for h in range(HEADS):
        at = h % 4 * BUCKETS
        bias_out[h : h + 1, :] = total[h // 4 : h // 4 + 1, at : at + BUCKETS]

    arrived(5)
    unpack(recv[5], first_two)
    unstage(stage_a, land, put_gk)
    unstage(stage_b, land, put_gv)
    arrived(6)
    unpack(recv[6], (((stage_a, 0), (stage_b, 0)),), 1)
    unstage(stage_a, land_last, end_gk)
    gone.append(leave(2, gk_out, gk_hbm))
    unstage(stage_b, land_last, end_gv)
    gone.append(leave(3, gv_out, gv_hbm))

    for copy in gone:
        copy.wait()
    for group in range(7):
        n = send[group].shape[0] // PEERS
        wait_bytes(send[group].at[pl.ds(n, (PEERS - 1) * n)], send_sem.at[group])
    k_halo.wait_send()
    v_halo.wait_send()
    g_halo.wait_send()
    for r in range(4):
        wait_bytes(red.at[r, pl.ds(0, rounds[r][0] - 1)], red_send.at[r])


def hand_over(*refs):
    for i in range(5):
        refs[5 + i][...] = refs[i][...]


def body(queries, keys, values, gates, cotangent, rel_bias, lengths, send_counts, block_pattern):
    vmem = pl.BlockSpec(memory_space=pltpu.VMEM)
    smem = pl.BlockSpec(memory_space=pltpu.SMEM)
    hbm = pl.BlockSpec(memory_space=pl.ANY)
    event = jax.ShapeDtypeStruct((ROWS, WIDTH), BF16)
    wide = pltpu.VMEM((ROWS, WIDTH), F32)
    low = pltpu.VMEM((ROWS, WIDTH), BF16)
    stage = pltpu.VMEM((LINES * CHUNKS, 128), F32)
    buffers = [pltpu.VMEM((PEERS * n, 16, 128), BF16) for n in (3, 2, 1, 1, 2, 2, 1)]
    results = pl.pallas_call(
        kernel,
        out_shape=(event, event, event, event, jax.ShapeDtypeStruct((HEADS, BUCKETS), F32)),
        in_specs=[hbm] * 5 + [smem] * 3 + [vmem],
        out_specs=(hbm,) * 4 + (vmem,),
        scratch_shapes=buffers * 2
        + [low] * 9
        + [stage, stage]
        + [pltpu.VMEM((LINES, ROWS), BF16)] * 2
        + [pltpu.VMEM((ROWS, LINES), BF16)] * 2
        + [pltpu.VMEM((ROWS, PEERS), BF16)]
        + [low] * 5
        + [low, pltpu.VMEM((ROWS + BLOCK, WIDTH), BF16), pltpu.VMEM((ROWS + BLOCK, WIDTH), BF16), wide]
        + [
            pltpu.VMEM((ROWS, 128), F32),
            pltpu.VMEM((2, HEADS, BLOCK, SPAN), BF16),
            pltpu.VMEM((2, HEADS, BLOCK, SPAN), F32),
            pltpu.VMEM((HEADS, BLOCK, SPAN), F32),
            pltpu.VMEM((2, BLOCK, SPAN), F32),
        ]
        + [wide, low, wide, wide]
        + [
            pltpu.VMEM((2, BLOCK, WIDTH), BF16),
            pltpu.VMEM((2, BLOCK, WIDTH), BF16),
            pltpu.VMEM((HEADS, BLOCK, SPAN), F32),
            pltpu.VMEM((HEADS * BUCKETS, SPAN), F32),
            pltpu.VMEM((4, 8, 8, 128), F32),
            pltpu.VMEM((4, 8, 128), F32),
            pltpu.SemaphoreType.DMA((7,)),
            pltpu.SemaphoreType.DMA((7,)),
            pltpu.SemaphoreType.DMA((3,)),
            pltpu.SemaphoreType.DMA((3,)),
            pltpu.SemaphoreType.DMA((4,)),
            pltpu.SemaphoreType.DMA((4,)),
            pltpu.SemaphoreType.REGULAR,
            pltpu.SemaphoreType.DMA((5,)),
            pltpu.SemaphoreType.DMA((4,)),
        ],
        compiler_params=pltpu.CompilerParams(
            collective_id=0, has_side_effects=True, vmem_limit_bytes=VMEM
        ),
    )(
        queries[0], keys[0], values[0], gates[0], cotangent[0],
        rel_bias, lengths, block_pattern, send_counts[0],
    )
    strips = [pl.BlockSpec((ROWS // 2, WIDTH), lambda i: (i, 0))] * 4
    strips.append(pl.BlockSpec((HEADS, BUCKETS), lambda i: (0, 0)))
    gq, gk, gv, gg, bias = pl.pallas_call(
        hand_over,
        out_shape=[jax.ShapeDtypeStruct(r.shape, r.dtype) for r in results],
        grid=(2,),
        in_specs=strips,
        out_specs=strips,
        compiler_params=pltpu.CompilerParams(vmem_limit_bytes=VMEM),
    )(*results)
    return gq[None], gk[None], gv[None], gg[None], bias


def solution(mesh):
    event = P("batch", "ctx", None)
    return jax.shard_map(
        body,
        mesh=mesh,
        in_specs=(event,) * 5 + (P(), P("batch", None), P("batch", None, None), event),
        out_specs=(event,) * 4 + (P(),),
        check_vma=False,
    )
```
